256 devices in a mesh: dp: 8 (over z), ctx: 8 (over x, core), exp: 4 (over y).
Axes of the slice: x: 4, y: 4, z: 8, core: 2. Of those that a mesh axis runs over, the one named last changes fastest.
Arguments:
- queries: bfloat16 [32768, 4096], P(('dp', 'ctx', 'exp')), parts along dimension 0, may hold values from -6 to 6
- key_rows: bfloat16 [32768, 4096], P(('dp', 'ctx', 'exp')), parts along dimension 0, may hold values from -6 to 6
- value_rows: bfloat16 [32768, 4096], P(('dp', 'ctx', 'exp')), parts along dimension 0, may hold values from -6 to 6
- residual: bfloat16 [32768, 4096], P(('dp', 'ctx', 'exp')), parts along dimension 0, may hold values from -18 to 18
- lambdas: float32 [32], replicated, may hold values from 0.2 to 0.8
- router: bfloat16 [4096, 8], replicated, may hold values from -0.09375 to 0.09375
- gate_proj: bfloat16 [8, 4096, 1024], P('ctx', None, 'exp'), may hold values from -0.09375 to 0.09375
- up_proj: bfloat16 [8, 4096, 1024], P('ctx', None, 'exp'), may hold values from -0.09375 to 0.09375
- down_proj: bfloat16 [8, 4096, 1024], P('ctx', None, 'exp'), may hold values from -0.1875 to 0.1875
- routes: int32 [32768, 2], P(('dp', 'ctx', 'exp')), parts along dimension 0, may hold values from 0 to 7, as said below
- capacity: int32 [256, 8], P(('dp', 'ctx', 'exp')), parts along dimension 0, may hold values from 18 to 36, as said below
Outputs:
- layer_out: bfloat16 [32768, 4096], P(('dp', 'ctx', 'exp')), parts along dimension 0
The draws below stay inside these ranges and needn't reach their ends.
There are 8 independent parts, one for each index of `dp`. The reference program is written for one: setup_inputs(seed, part) draws one part's arguments, and reference() takes and returns one part's arrays. A program takes and returns all parts, laid end to end along the dimension named above; an argument that names none is the same for every part. Nothing has to cross between parts.
Inputs may be any that keep to these rules, and one draw needn't show every extreme that they name: `routes`: each row names two different experts. For one expert H, drawn from the seed, at least 36 tokens of every block of 128 tokens name it. capacity[b, H] = 36 for every block b, H being the expert of the routes' promise.
All inputs are finite; a program needn't handle non-finite values.
Results may differ from the reference program's by a relative error of at most 0.0042.
Values may be sent and summed in bfloat16 or wider, within the bound.
A program may use at most 128 MiB of HBM per device.

```python
import math
import jax
import jax.numpy as jnp
from jax import lax

D = 4096
HEADS = 32
HD = 64
FF = 1024
TOK_DEV = 128
DEVS = 32
SEQ = 4096
EXPERTS = 8
FF_DEV = 256
CAP = 36


def hot_expert(key):
    return jax.random.randint(jax.random.fold_in(key, 97), (), 0, EXPERTS)


def draw_queries(key, part):
    own_key = jax.random.fold_in(key, 3)
    result = jnp.clip(jax.random.normal(own_key, (SEQ, D), jnp.float32), -4.0, 4.0)
    return result.astype(jnp.bfloat16)


def draw_key_rows(key, part):
    own_key = jax.random.fold_in(key, 4)
    result = jnp.clip(jax.random.normal(own_key, (SEQ, D), jnp.float32), -4.0, 4.0)
    return result.astype(jnp.bfloat16)


def draw_residual(key, part):
    own_key = jax.random.fold_in(key, 5)
    key_rows, key_cols, key_noise = jax.random.split(own_key, 3)
    row_scale = 0.5 * jnp.exp(jax.random.uniform(key_rows, (SEQ, 1), jnp.float32, 0.0, math.log(4.0)))
    col_scale = 0.3 * jnp.exp(jax.random.uniform(key_cols, (1, D), jnp.float32, 0.0, math.log(10.0)))
    noise = jnp.clip(jax.random.normal(key_noise, (SEQ, D), jnp.float32), -3.0, 3.0)
    result = noise * row_scale * col_scale
    return result.astype(jnp.bfloat16)


def draw_routes(key, part):
    hot = hot_expert(key)
    own_key = jax.random.fold_in(key, 1)
    key_rank, key_first, key_second, key_turn = jax.random.split(own_key, 4)
    ranking = jax.random.randint(key_rank, (DEVS, TOK_DEV), 0, 1 << 20) * TOK_DEV + jnp.arange(TOK_DEV)[None, :]
    ordering = jnp.argsort(ranking, axis=1)
    placing = jnp.argsort(ordering, axis=1)
    chosen = placing < CAP
    skewed = jnp.minimum(jax.random.randint(key_first, (DEVS, TOK_DEV), 0, EXPERTS), jax.random.randint(jax.random.fold_in(key_first, 5), (DEVS, TOK_DEV), 0, EXPERTS))
    rotate = jax.random.randint(key_turn, (), 0, EXPERTS)
    first_route = jnp.where(chosen, hot, (skewed + rotate) % EXPERTS)
    second_route = (first_route + 1 + jax.random.randint(key_second, (DEVS, TOK_DEV), 0, EXPERTS - 1)) % EXPERTS
    flipped = jax.random.randint(jax.random.fold_in(key_turn, 7), (DEVS, TOK_DEV), 0, 2) == 1
    left_route = jnp.where(flipped, second_route, first_route)
    right_route = jnp.where(flipped, first_route, second_route)
    return jnp.stack([left_route, right_route], axis=-1).reshape(SEQ, 2).astype(jnp.int32)


def draw_capacity(key, part):
    hot = hot_expert(key)
    own_key = jax.random.fold_in(key, 2)
    counts = jax.random.randint(own_key, (DEVS, EXPERTS), (CAP + 1) // 2, CAP + 1)
    return jnp.where(jnp.arange(EXPERTS)[None, :] == hot, CAP, counts).astype(jnp.int32)


def steps_of(key, shape, cuts, smallest, high):
    def one(dim, parts):
        steps = jax.random.uniform(jax.random.fold_in(jax.random.fold_in(key, 6), dim), (parts,), jnp.float32, smallest / len(cuts), high / len(cuts))
        return jnp.repeat(jnp.exp(steps), shape[dim] // parts).reshape((-1,) + (1,) * (len(shape) - dim - 1))

    factor_of = one(*cuts[0])
    for cut in cuts[1:]:
        factor_of = factor_of * one(*cut)
    return factor_of


def normal_values(rng, shape, scale, bound, cuts=(), kind=jnp.bfloat16):
    values = jax.random.normal(rng, shape, jnp.float32) * scale
    if len(cuts) > 0:
        values = steps_of(rng, shape, cuts, -0.22, 0.18) * values
    return jnp.clip(values, min=-bound, max=bound).astype(kind)


def setup_inputs(seed: int = 0, part: int = 0) -> dict:
    key_of = jax.random.split(jax.random.key(seed), 12)
    part_splits = jax.random.split(jax.random.fold_in(key_of[11], part), 12)
    return {
        "queries": draw_queries(jax.random.fold_in(jax.random.fold_in(key_of[11], part), 71), part),
        "key_rows": draw_key_rows(jax.random.fold_in(jax.random.fold_in(key_of[11], part), 71), part),
        "value_rows": normal_values(part_splits[2], (SEQ, D), 1.0, 6.0, ((0, 32),)),
        "residual": draw_residual(jax.random.fold_in(jax.random.fold_in(key_of[11], part), 71), part),
        "lambdas": jnp.clip(jnp.exp(jax.random.uniform(key_of[4], (HEADS,), jnp.float32, math.log(0.2), math.log(0.8))), 0.2, 0.8),
        "router": normal_values(key_of[5], (D, EXPERTS), D ** -0.5, 0.09375),
        "gate_proj": normal_values(key_of[6], (EXPERTS, D, FF), D ** -0.5, 0.09375, ((0, 8), (2, 4))),
        "up_proj": normal_values(key_of[7], (EXPERTS, D, FF), D ** -0.5, 0.09375, ((0, 8), (2, 4))),
        "down_proj": normal_values(key_of[8], (EXPERTS, D, FF), FF ** -0.5, 0.1875, ((0, 8), (2, 4))),
        "routes": draw_routes(jax.random.fold_in(jax.random.fold_in(key_of[11], part), 71), part),
        "capacity": draw_capacity(jax.random.fold_in(jax.random.fold_in(key_of[11], part), 71), part),
    }


epsilon = 1e-05
out_scale = 0.8

def head_mix(operands):
    q_pair, k_pair, v_head, weight_two = operands
    length = q_pair.shape[0]
    position = jnp.arange(length)
    allowed = position[None, :] <= position[:, None]
    score_scale = 1.0 / math.sqrt(HD)
    softmaxes = []
    for map_index in range(2):
        first_col = map_index * HD
        scores = jnp.dot(q_pair[:, first_col:first_col + HD], k_pair[:, first_col:first_col + HD].T, preferred_element_type=jnp.float32) * score_scale
        scores = jnp.where(allowed, scores, -jnp.inf)
        largest = lax.optimization_barrier(jnp.max(scores, axis=1, keepdims=True))
        raised = jnp.exp(scores - largest)
        softmaxes.append(raised / lax.optimization_barrier(jnp.sum(raised, axis=1, keepdims=True)))
    weights = (softmaxes[0] - weight_two * softmaxes[1]).astype(jnp.bfloat16)
    mixed_rows = jnp.dot(weights, v_head, preferred_element_type=jnp.float32)
    normed = out_scale * mixed_rows * lax.rsqrt(lax.optimization_barrier(jnp.mean(mixed_rows * mixed_rows, axis=1, keepdims=True)) + epsilon)
    return normed.astype(jnp.bfloat16)

def expert_mix(operands):
    token_rows, gate_w, up_w, down_w = operands
    gate_out = jnp.dot(token_rows, gate_w, preferred_element_type=jnp.float32)
    up_out = jnp.dot(token_rows, up_w, preferred_element_type=jnp.float32)
    hidden = (jax.nn.silu(gate_out) * up_out).astype(jnp.bfloat16)
    summed = jnp.zeros((token_rows.shape[0], D), jnp.float32)
    for group_index in range(FF // FF_DEV):
        group_start = group_index * FF_DEV
        part_out = jnp.dot(hidden[:, group_start:group_start + FF_DEV], down_w[:, group_start:group_start + FF_DEV].T, preferred_element_type=jnp.float32).astype(jnp.bfloat16)
        summed = summed + part_out.astype(jnp.float32)
    return summed.astype(jnp.bfloat16)

def reference(queries, key_rows, value_rows, residual, lambdas, router, gate_proj, up_proj, down_proj, routes, capacity):
    span = 2 * HD
    query_heads = queries.reshape(SEQ, HEADS, span).transpose(1, 0, 2)
    key_heads = key_rows.reshape(SEQ, HEADS, span).transpose(1, 0, 2)
    value_heads = value_rows.reshape(SEQ, HEADS, span).transpose(1, 0, 2)
    head_rows = lax.map(head_mix, (query_heads, key_heads, value_heads, lambdas))
    head_out = head_rows.transpose(1, 0, 2).reshape(SEQ, D)
    attended = residual.astype(jnp.float32) + head_out.astype(jnp.float32)
    normed = (attended * lax.rsqrt(lax.optimization_barrier(jnp.mean(attended * attended, axis=1, keepdims=True)) + epsilon)).astype(jnp.bfloat16)
    logits = jnp.dot(normed, router, preferred_element_type=jnp.float32)
    chosen_mask = routes[:, :, None] == jnp.arange(EXPERTS, dtype=jnp.int32)[None, None, :]
    sigmoid_all = jax.nn.sigmoid(logits)
    picked_sig = lax.optimization_barrier(jnp.sum(jnp.where(chosen_mask, sigmoid_all[:, None, :], 0.0), axis=2))
    gates = picked_sig / lax.optimization_barrier(jnp.sum(picked_sig, axis=1, keepdims=True))
    one_hot = chosen_mask.reshape(DEVS, TOK_DEV * 2, EXPERTS).astype(jnp.int32)
    earlier = jnp.cumsum(one_hot, axis=1) - one_hot
    position = lax.optimization_barrier(jnp.sum(earlier * one_hot, axis=2))
    allowance = lax.optimization_barrier(jnp.sum(capacity[:, None, :] * one_hot, axis=2))
    kept = position < allowance
    expert_ids = routes.reshape(DEVS, TOK_DEV * 2)
    device_ids = jnp.arange(DEVS, dtype=jnp.int32)[:, None]
    full_slots = EXPERTS * DEVS * CAP
    target = jnp.where(kept, (expert_ids * DEVS + device_ids) * CAP + position, full_slots).reshape(-1).astype(jnp.int32)
    token_rows = jnp.repeat(normed, 2, axis=0)
    buffer = jnp.zeros((full_slots, D), jnp.bfloat16).at[target].set(token_rows, mode='drop')
    results = lax.map(expert_mix, (buffer.reshape(EXPERTS, DEVS * CAP, D), gate_proj, up_proj, down_proj))
    results = results.reshape(full_slots, D)
    picked = results[jnp.minimum(target, full_slots - 1)]
    share = jnp.where(kept.reshape(-1), gates.reshape(-1), 0.0)
    expert_sum = lax.optimization_barrier(jnp.sum((picked.astype(jnp.float32) * share[:, None]).reshape(SEQ, 2, D), axis=1))
    return (attended + expert_sum).astype(jnp.bfloat16)
```

```python
import functools
import math

import jax
import jax.numpy as jnp
from jax import lax
from jax.experimental import pallas as pl
from jax.experimental.pallas import tpu as pltpu
from jax.sharding import PartitionSpec as P

EPSILON = 1e-05
OUT_SCALE = 0.8
LOG2E = math.log2(math.e)
LOW = -1e30
LANES = 128
SLOTS = 40
MIB = 1024 * 1024
contract_last = (((1,), (1,)), ((), ()))
contract_first = (((0,), (0,)), ((), ()))


def attention_kernel(bq, bk, lam_ref, qkv_ref, o_ref, kk, vv, qq, acc, largest):
    sources, _, rows, width = qkv_ref.shape
    length = sources * rows
    half = width // 2
    step_index = pl.program_id(0)

    @pl.when(step_index == 0)
    def _():
        keys = qkv_ref[:, 1].reshape(length, width)
        kk[:, :width] = keys
        kk[:, width:] = keys
        vv[:, :width] = qkv_ref[:, 2].reshape(length, width)
        vv[:, width:] = jnp.ones((length, width), vv.dtype)

    per = bq // rows
    q = qkv_ref[pl.ds(step_index * per, per), 0].reshape(bq, width)
    q = q.astype(jnp.float32) * (LOG2E / math.sqrt(half))
    hi = q.astype(jnp.bfloat16)
    lo = (q - hi.astype(jnp.float32)).astype(jnp.bfloat16)
    first = lax.broadcasted_iota(jnp.int32, (bq, width), 1) < half
    zero = jnp.zeros((bq, width), jnp.bfloat16)
    qq[:bq, :width] = jnp.where(first, hi, zero)
    qq[:bq, width:] = jnp.where(first, lo, zero)
    qq[bq:, :width] = jnp.where(first, zero, hi)
    qq[bq:, width:] = jnp.where(first, zero, lo)
    acc[...] = jnp.zeros_like(acc)
    largest[...] = jnp.full_like(largest, LOW)

    def chunk(j, masked):
        s = lax.dot_general(
            qq[...], kk[pl.ds(j * bk, bk), :], contract_last, preferred_element_type=jnp.float32
        )
        if masked:
            row = step_index * bq + lax.broadcasted_iota(jnp.int32, (bq, bk), 0)
            col = j * bk + lax.broadcasted_iota(jnp.int32, (bq, bk), 1)
            allowed = col <= row
            s = jnp.where(jnp.concatenate([allowed, allowed], axis=0), s, LOW)
        old = largest[...]
        new = jnp.maximum(old, jnp.max(s, axis=1, keepdims=True))
        largest[...] = new
        shrink = jnp.exp2(old - new)
        raised = jnp.exp2(s - new[:, :1]).astype(jnp.bfloat16)
        part = jnp.dot(raised, vv[pl.ds(j * bk, bk), :], preferred_element_type=jnp.float32)
        acc[:, :width] = acc[:, :width] * shrink + part[:, :width]
        acc[:, width:] = acc[:, width:] * shrink + part[:, width:]

    full = (step_index * bq) // bk

    def body(j, carried):
        chunk(j, False)
        return carried

    lax.fori_loop(0, full, body, 0)
    chunk(full, True)
    one = acc[:bq, :width] / acc[:bq, width:]
    two = acc[bq:, :width] / acc[bq:, width:]
    mixed = one - lam_ref[0] * two
    mean = jnp.mean(mixed * mixed, axis=1, keepdims=True)
    out = (OUT_SCALE * mixed * lax.rsqrt(mean + EPSILON)).astype(o_ref.dtype)
    o_ref[...] = out.reshape(o_ref.shape)


def attention(qkv, lam, bq=512, bk=1024):
    sources, _, rows, width = qkv.shape
    length = sources * rows
    per = bq // rows
    return pl.pallas_call(
        functools.partial(attention_kernel, bq, bk),
        grid=(length // bq,),
        out_shape=jax.ShapeDtypeStruct((sources, rows, width), jnp.bfloat16),
        in_specs=[
            pl.BlockSpec(memory_space=pltpu.SMEM),
            pl.BlockSpec(memory_space=pltpu.VMEM),
        ],
        out_specs=pl.BlockSpec((per, rows, width), lambda i: (i, 0, 0)),
        scratch_shapes=[
            pltpu.VMEM((length, 2 * width), jnp.bfloat16),
            pltpu.VMEM((length, 2 * width), jnp.bfloat16),
            pltpu.VMEM((2 * bq, 2 * width), jnp.bfloat16),
            pltpu.VMEM((2 * bq, 2 * width), jnp.float32),
            pltpu.VMEM((2 * bq, width), jnp.float32),
        ],
        compiler_params=pltpu.CompilerParams(vmem_limit_bytes=48 * MIB),
        cost_estimate=pl.CostEstimate(
            flops=6 * length * length * width, bytes_accessed=4 * MIB, transcendentals=length * length
        ),
        name="attention",
    )(lam, qkv)


def attend_columns(res_ref, heads_ref, h):
    columns = slice(h * LANES, (h + 1) * LANES)
    return res_ref[:, columns].astype(jnp.float32) + heads_ref[h].astype(jnp.float32)


def route_kernel(res_ref, heads_ref, router_ref, routes_ref, cap_ref, buf_ref, gate_ref, normed):
    heads, tokens, width = heads_ref.shape
    experts = router_ref.shape[0]
    square = jnp.zeros((tokens, width), jnp.float32)
    for h in range(heads):
        block = attend_columns(res_ref, heads_ref, h)
        square = square + block * block
    mean = jnp.sum(square, axis=1, keepdims=True) / (heads * width)
    factor = lax.rsqrt(mean + EPSILON)
    for h in range(heads):
        block = attend_columns(res_ref, heads_ref, h)
        normed[:, h * width : (h + 1) * width] = (block * factor).astype(jnp.bfloat16)
    logits = lax.dot_general(
        router_ref[...], normed[...], contract_last, preferred_element_type=jnp.float32
    )
    sig = 1.0 / (1.0 + jnp.exp(-logits))
    expert = lax.broadcasted_iota(jnp.int32, (experts, tokens), 0)
    named = (routes_ref[0:1, :] == expert) | (routes_ref[1:2, :] == expert)
    picked = jnp.where(named, sig, 0.0)
    gates = picked / jnp.sum(picked, axis=0, keepdims=True)
    before = lax.broadcasted_iota(jnp.int32, (tokens, tokens), 0) < lax.broadcasted_iota(
        jnp.int32, (tokens, tokens), 1
    )
    position = jnp.dot(
        named.astype(jnp.bfloat16), before.astype(jnp.bfloat16), preferred_element_type=jnp.float32
    )
    kept = named & (position < cap_ref[...].astype(jnp.float32))
    position = jnp.where(kept, position, -1.0).astype(jnp.int32)
    slot = lax.broadcasted_iota(jnp.int32, (SLOTS, tokens), 0)
    chosen = [slot == position[e : e + 1, :] for e in range(experts)]
    one_hot = jnp.concatenate([jnp.where(c, 1.0, 0.0) for c in chosen], axis=0)
    gate_ref[...] = jnp.concatenate(
        [jnp.where(chosen[e], gates[e : e + 1, :], 0.0) for e in range(experts)], axis=0
    )
    one_hot = one_hot.astype(jnp.bfloat16)
    for h in range(0, heads * width, 512):
        buf_ref[:, h : h + 512] = jnp.dot(
            one_hot, normed[:, h : h + 512], preferred_element_type=jnp.float32
        ).astype(jnp.bfloat16)


def route(residual, heads, router, routes, capacity):
    tokens, width = residual.shape
    experts = router.shape[0]
    slots = experts * SLOTS
    return pl.pallas_call(
        route_kernel,
        out_shape=(
            jax.ShapeDtypeStruct((slots, width), jnp.bfloat16),
            jax.ShapeDtypeStruct((slots, tokens), jnp.float32),
        ),
        scratch_shapes=[pltpu.VMEM((tokens, width), jnp.bfloat16)],
        compiler_params=pltpu.CompilerParams(vmem_limit_bytes=48 * MIB),
        name="route",
    )(residual, heads, router, routes, capacity)


def expert_kernel(x_ref, gate_ref, up_ref, down_ref, o_ref, acc):
    group = pl.program_id(0)
    x = x_ref[...]
    gate_out = jnp.dot(x, gate_ref[...], preferred_element_type=jnp.float32)
    up_out = jnp.dot(x, up_ref[...], preferred_element_type=jnp.float32)
    hidden = (gate_out / (1.0 + jnp.exp(-gate_out)) * up_out).astype(jnp.bfloat16)
    width = x_ref.shape[1]
    for c in range(0, width, 512):
        part = lax.dot_general(
            hidden, down_ref[c : c + 512, :], contract_last, preferred_element_type=jnp.float32
        ).astype(jnp.bfloat16).astype(jnp.float32)

        @pl.when(group == 0)
        def _():
            acc[:, c : c + 512] = part

        @pl.when(group > 0)
        def _():
            acc[:, c : c + 512] += part

    @pl.when(group == pl.num_programs(0) - 1)
    def _():
        o_ref[...] = acc[...].astype(o_ref.dtype)


def expert(x, gate_w, up_w, down_w):
    rows, width = x.shape
    groups, _, hidden = gate_w.shape
    weight = pl.BlockSpec((None, width, hidden), lambda g: (g, 0, 0))
    return pl.pallas_call(
        expert_kernel,
        grid=(groups,),
        out_shape=jax.ShapeDtypeStruct((rows, width), jnp.bfloat16),
        in_specs=[pl.BlockSpec((rows, width), lambda g: (0, 0)), weight, weight, weight],
        out_specs=pl.BlockSpec((rows, width), lambda g: (0, 0)),
        scratch_shapes=[pltpu.VMEM((rows, width), jnp.float32)],
        compiler_params=pltpu.CompilerParams(vmem_limit_bytes=56 * MIB),
        cost_estimate=pl.CostEstimate(
            flops=6 * rows * width * hidden * groups, bytes_accessed=30 * MIB, transcendentals=rows * hidden * groups
        ),
        name="experts",
    )(x, gate_w, up_w, down_w)


def combine_kernel(res_ref, heads_ref, back_ref, gate_ref, o_ref):
    heads = heads_ref.shape[0]
    gates = gate_ref[...]
    hi = gates.astype(jnp.bfloat16)
    lo = (gates - hi.astype(jnp.float32)).astype(jnp.bfloat16)
    for h in range(heads):
        columns = slice(h * LANES, (h + 1) * LANES)
        back = back_ref[:, columns]
        total = lax.dot_general(hi, back, contract_first, preferred_element_type=jnp.float32)
        total += lax.dot_general(lo, back, contract_first, preferred_element_type=jnp.float32)
        o_ref[:, columns] = (attend_columns(res_ref, heads_ref, h) + total).astype(o_ref.dtype)


def combine(residual, heads, back, gates):
    return pl.pallas_call(
        combine_kernel,
        out_shape=jax.ShapeDtypeStruct(residual.shape, jnp.bfloat16),
        compiler_params=pltpu.CompilerParams(vmem_limit_bytes=48 * MIB),
        name="combine",
    )(residual, heads, back, gates)


def shards(
    queries, key_rows, value_rows, residual, lambdas, router, gate_proj, up_proj, down_proj, routes, capacity
):
    tokens, width = queries.shape
    experts = router.shape[1]
    gate_all = lax.all_gather(gate_proj[0], "exp")
    up_all = lax.all_gather(up_proj[0], "exp")
    down_all = lax.all_gather(down_proj[0], "exp")

    heads = lambdas.shape[0]
    qkv = jnp.stack([queries, key_rows, value_rows]).reshape(3, tokens, heads, LANES)
    qkv = lax.all_to_all(
        qkv.transpose(2, 0, 1, 3), ("ctx", "exp"), split_axis=0, concat_axis=0, tiled=True
    )
    lam = lax.dynamic_slice_in_dim(lambdas, lax.axis_index(("ctx", "exp")), 1)
    mixed = attention(qkv, lam)
    mixed = lax.all_to_all(mixed, ("ctx", "exp"), split_axis=0, concat_axis=0, tiled=True)

    buffer, gates = route(residual, mixed, router.T, routes.T, capacity.T)
    buffer = lax.all_to_all(
        buffer.reshape(experts, SLOTS, width), "ctx", split_axis=0, concat_axis=0, tiled=True
    )
    results = expert(buffer.reshape(experts * SLOTS, width), gate_all, up_all, down_all)
    back = lax.all_to_all(
        results.reshape(experts, SLOTS, width), "ctx", split_axis=0, concat_axis=0, tiled=True
    )
    return combine(residual, mixed, back.reshape(experts * SLOTS, width), gates)


def solution(mesh):
    rows = P(("dp", "ctx", "exp"), None)
    weights = P("ctx", None, "exp")
    placed = (rows, rows, rows, rows, P(), P(), weights, weights, weights, rows, rows)
    return jax.shard_map(shards, mesh=mesh, in_specs=placed, out_specs=rows, check_vma=False)
```

```python
import functools
import math

import jax
import jax.numpy as jnp
from jax import lax
from jax.experimental import pallas as pl
from jax.experimental.pallas import tpu as pltpu
from jax.sharding import PartitionSpec as P

EPSILON = 1e-05
OUT_SCALE = 0.8
LOG2E = math.log2(math.e)
LOW = -1e30
LANES = 128
SLOTS = 40
MIB = 1024 * 1024
MESH = pl.DeviceIdType.MESH
contract_last = (((1,), (1,)), ((), ()))
contract_first = (((0,), (0,)), ((), ()))


def relative(ctx=0, exp=0, dp=0):
    def place(axis, step):
        size = lax.axis_size(axis)
        return lax.rem(lax.axis_index(axis) + step + size, size)

    return {"dp": place("dp", dp), "ctx": place("ctx", ctx), "exp": place("exp", exp)}


def front_kernel(
    bq, bk, lam_ref, q_ref, k_ref, v_ref, gate_ref, up_ref, down_ref, heads_ref, gate_all, up_all, down_all,
    qkv, mixed, kk, vv, qq, acc, largest, qkv_send, qkv_recv, out_send, out_recv, w_send, w_recv,
):
    _, sources, rows, width = qkv.shape
    length = sources * rows
    half = width // 2
    fan = lax.axis_size("exp")
    me = lax.axis_index("ctx") * fan + lax.axis_index("exp")
    parity = lax.rem(lax.axis_index("dp"), 2)

    def member(index):
        return {"dp": lax.axis_index("dp"), "ctx": lax.div(index, fan), "exp": lax.rem(index, fan)}

    barrier = pltpu.get_barrier_semaphore()

    def greet(step, carried):
        pl.semaphore_signal(
            barrier, inc=1, device_id=member(lax.rem(me + step, sources)), device_id_type=MESH
        )
        return carried

    lax.fori_loop(1, sources, greet, 0)
    pl.semaphore_signal(barrier, inc=1, device_id=relative(dp=1), device_id_type=MESH)
    pl.semaphore_signal(barrier, inc=1, device_id=relative(dp=-1), device_id_type=MESH)
    pl.semaphore_wait(barrier, sources + 1)

    inputs = (q_ref, k_ref, v_ref)

    def send_heads(step, carried):
        target = lax.rem(me + step, sources)
        columns = pl.ds(pl.multiple_of(target * width, width), width)
        for which in range(3):
            pltpu.make_async_remote_copy(
                src_ref=inputs[which].at[:, columns],
                dst_ref=qkv.at[which, me],
                send_sem=qkv_send,
                recv_sem=qkv_recv,
                device_id=member(target),
                device_id_type=MESH,
            ).start()
        return carried

    lax.fori_loop(1, sources, send_heads, 0)
    own = pl.ds(pl.multiple_of(me * width, width), width)
    for which in range(3):
        pltpu.make_async_copy(inputs[which].at[:, own], qkv.at[which, me], qkv_recv).start()

    weights = (gate_ref, up_ref, down_ref)
    gathered = (gate_all, up_all, down_all)
    quarter = gate_ref.shape[0] // 4

    def chunk_rows(which_half, part):
        return pl.ds(pl.multiple_of((which_half * 2 + part) * quarter, quarter), quarter)

    def transfer(array, slot, part, along_dp, src, forward):
        ways = relative(dp=1 if part == 0 else -1) if along_dp else relative(exp=1 if forward else -1)
        number = ((array * 3 + slot) * 2 + part) * 2 + (1 if along_dp else 0)
        return pltpu.make_async_remote_copy(
            src_ref=src,
            dst_ref=gathered[array].at[slot, chunk_rows(parity, part)],
            send_sem=w_send.at[number],
            recv_sem=w_recv.at[number],
            device_id=ways,
            device_id_type=MESH,
        )

    def arrived(array, slot, part, along_dp):
        number = ((array * 3 + slot) * 2 + part) * 2 + (1 if along_dp else 0)
        rows_here = chunk_rows(1 - parity if along_dp else parity, part)
        block = gathered[array].at[slot, rows_here]
        pltpu.make_async_copy(block, block, w_recv.at[number]).wait()

    def own_copy(array, slot, part):
        return transfer(
            array, slot, part, False, weights[array].at[chunk_rows(parity, part)], slot == 1
        )

    def across(array, part):
        slot = 1 if part == 0 else 0
        return transfer(
            array, 2, part, False, gathered[array].at[slot, chunk_rows(parity, part)], part == 0
        )

    def along(array, slot, part):
        return transfer(
            array, slot, part, True, gathered[array].at[slot, chunk_rows(parity, part)], None
        )

    def first(array):
        for part in range(2):
            own_copy(array, 1, part).start()
            own_copy(array, 0, 1 - part).start()

    def second(array):
        arrived(array, 1, 0, False)
        across(array, 0).start()
        along(array, 1, 0).start()
        arrived(array, 0, 1, False)
        across(array, 1).start()
        along(array, 0, 1).start()
        arrived(array, 1, 1, False)
        along(array, 1, 1).start()
        arrived(array, 0, 0, False)
        along(array, 0, 0).start()

    def third(array):
        arrived(array, 2, 0, False)
        along(array, 2, 0).start()
        arrived(array, 2, 1, False)
        along(array, 2, 1).start()

    def last(array):
        for slot in range(3):
            for part in range(2):
                arrived(array, slot, part, True)
                along(array, slot, part).wait_send()
        for part in range(2):
            own_copy(array, 0, part).wait_send()
            own_copy(array, 1, part).wait_send()
            across(array, part).wait_send()

    first(0)
    first(1)

    pltpu.make_async_copy(qkv, qkv, qkv_recv).wait()
    keys = qkv[1].reshape(length, width)
    kk[:, :width] = keys
    kk[:, width:] = keys
    vv[:, :width] = qkv[2].reshape(length, width)
    vv[:, width:] = jnp.ones((length, width), vv.dtype)

    per = bq // rows
    lam = lam_ref[me]

    def query_block(i, carried):
        @pl.when(i == 2)
        def _():
            second(0)
            first(2)

        @pl.when(i == 4)
        def _():
            third(0)

        @pl.when(i == 5)
        def _():
            second(1)

        @pl.when(i == 6)
        def _():
            third(1)

        q = qkv[0, pl.ds(i * per, per)].reshape(bq, width)
        q = q.astype(jnp.float32) * (LOG2E / math.sqrt(half))
        hi = q.astype(jnp.bfloat16)
        lo = (q - hi.astype(jnp.float32)).astype(jnp.bfloat16)
        lower = lax.broadcasted_iota(jnp.int32, (bq, width), 1) < half
        zero = jnp.zeros((bq, width), jnp.bfloat16)
        qq[:bq, :width] = jnp.where(lower, hi, zero)
        qq[:bq, width:] = jnp.where(lower, lo, zero)
        qq[bq:, :width] = jnp.where(lower, zero, hi)
        qq[bq:, width:] = jnp.where(lower, zero, lo)
        acc[...] = jnp.zeros_like(acc)
        largest[...] = jnp.full_like(largest, LOW)

        def chunk(j, masked):
            keys_here = pl.ds(pl.multiple_of(j * bk, bk), bk)
            s = lax.dot_general(
                qq[...], kk[keys_here, :], contract_last, preferred_element_type=jnp.float32
            )
            if masked:
                row = i * bq + lax.broadcasted_iota(jnp.int32, (bq, bk), 0)
                col = j * bk + lax.broadcasted_iota(jnp.int32, (bq, bk), 1)
                allowed = col <= row
                s = jnp.where(jnp.concatenate([allowed, allowed], axis=0), s, LOW)
            old = largest[...]
            new = jnp.maximum(old, jnp.max(s, axis=1, keepdims=True))
            largest[...] = new
            shrink = jnp.exp2(old - new)
            raised = jnp.exp2(s - new[:, :1]).astype(jnp.bfloat16)
            part = jnp.dot(raised, vv[keys_here, :], preferred_element_type=jnp.float32)
            acc[:, :width] = acc[:, :width] * shrink + part[:, :width]
            acc[:, width:] = acc[:, width:] * shrink + part[:, width:]

        full = lax.div(i * bq, bk)

        def body(j, inner):
            chunk(j, False)
            return inner

        lax.fori_loop(0, full, body, 0)
        chunk(full, True)
        one = acc[:bq, :width] / acc[:bq, width:]
        two = acc[bq:, :width] / acc[bq:, width:]
        blend = one - lam * two
        mean = jnp.mean(blend * blend, axis=1, keepdims=True)
        out = (OUT_SCALE * blend * lax.rsqrt(mean + EPSILON)).astype(mixed.dtype)
        mixed[pl.ds(i * per, per)] = out.reshape(per, rows, width)

        def send_rows(r, inner):
            target = i * per + r

            @pl.when(target != me)
            def _():
                pltpu.make_async_remote_copy(
                    src_ref=mixed.at[target],
                    dst_ref=heads_ref.at[me],
                    send_sem=out_send,
                    recv_sem=out_recv,
                    device_id=member(target),
                    device_id_type=MESH,
                ).start()

            @pl.when(target == me)
            def _():
                pltpu.make_async_copy(mixed.at[target], heads_ref.at[me], out_recv).start()

            return inner

        lax.fori_loop(0, per, send_rows, 0)
        return carried

    lax.fori_loop(0, length // bq, query_block, 0)
    second(2)
    third(2)
    others = pl.ds(0, sources - 1)
    for which in range(3):
        pltpu.make_async_copy(qkv.at[which, others], qkv.at[which, others], qkv_send).wait()
    pltpu.make_async_copy(mixed.at[others], mixed.at[others], out_send).wait()
    pltpu.make_async_copy(heads_ref, heads_ref, out_recv).wait()
    for array in range(3):
        last(array)


def front(lambdas, queries, key_rows, value_rows, gate_w, up_w, down_w, bq=512, bk=1024):
    rows, total = queries.shape
    width = LANES
    heads = total // width
    length = heads * rows
    anywhere = pl.BlockSpec(memory_space=pl.ANY)
    others = jax.ShapeDtypeStruct((lax.axis_size("exp") - 1, *gate_w.shape), gate_w.dtype)
    copies = 3 * 3 * 2 * 2
    return pl.pallas_call(
        functools.partial(front_kernel, bq, bk),
        out_shape=(jax.ShapeDtypeStruct((heads, rows, width), jnp.bfloat16), others, others, others),
        in_specs=[pl.BlockSpec(memory_space=pltpu.SMEM)] + [anywhere] * 6,
        out_specs=(anywhere,) * 4,
        scratch_shapes=[
            pltpu.VMEM((3, heads, rows, width), jnp.bfloat16),
            pltpu.VMEM((heads, rows, width), jnp.bfloat16),
            pltpu.VMEM((length, 2 * width), jnp.bfloat16),
            pltpu.VMEM((length, 2 * width), jnp.bfloat16),
            pltpu.VMEM((2 * bq, 2 * width), jnp.bfloat16),
            pltpu.VMEM((2 * bq, 2 * width), jnp.float32),
            pltpu.VMEM((2 * bq, width), jnp.float32),
            pltpu.SemaphoreType.DMA,
            pltpu.SemaphoreType.DMA,
            pltpu.SemaphoreType.DMA,
            pltpu.SemaphoreType.DMA,
            pltpu.SemaphoreType.DMA((copies,)),
            pltpu.SemaphoreType.DMA((copies,)),
        ],
        compiler_params=pltpu.CompilerParams(
            vmem_limit_bytes=56 * MIB, collective_id=0, has_side_effects=True
        ),
        name="front",
    )(lambdas, queries, key_rows, value_rows, gate_w, up_w, down_w)


def attend_columns(res_ref, heads_ref, h):
    columns = slice(h * LANES, (h + 1) * LANES)
    return res_ref[:, columns].astype(jnp.float32) + heads_ref[h].astype(jnp.float32)


def route_kernel(res_ref, heads_ref, router_ref, routes_ref, cap_ref, buf_ref, gate_ref, normed):
    heads, tokens, width = heads_ref.shape
    experts = router_ref.shape[0]
    square = jnp.zeros((tokens, width), jnp.float32)
    for h in range(heads):
        block = attend_columns(res_ref, heads_ref, h)
        square = square + block * block
    mean = jnp.sum(square, axis=1, keepdims=True) / (heads * width)
    factor = lax.rsqrt(mean + EPSILON)
    for h in range(heads):
        block = attend_columns(res_ref, heads_ref, h)
        normed[:, h * width : (h + 1) * width] = (block * factor).astype(jnp.bfloat16)
    logits = lax.dot_general(
        router_ref[...], normed[...], contract_last, preferred_element_type=jnp.float32
    )
    sig = 1.0 / (1.0 + jnp.exp(-logits))
    expert = lax.broadcasted_iota(jnp.int32, (experts, tokens), 0)
    named = (routes_ref[0:1, :] == expert) | (routes_ref[1:2, :] == expert)
    picked = jnp.where(named, sig, 0.0)
    gates = picked / jnp.sum(picked, axis=0, keepdims=True)
    before = lax.broadcasted_iota(jnp.int32, (tokens, tokens), 0) < lax.broadcasted_iota(
        jnp.int32, (tokens, tokens), 1
    )
    position = jnp.dot(
        named.astype(jnp.bfloat16), before.astype(jnp.bfloat16), preferred_element_type=jnp.float32
    )
    kept = named & (position < cap_ref[...].astype(jnp.float32))
    position = jnp.where(kept, position, -1.0).astype(jnp.int32)
    slot = lax.broadcasted_iota(jnp.int32, (SLOTS, tokens), 0)
    chosen = [slot == position[e : e + 1, :] for e in range(experts)]
    one_hot = jnp.concatenate([jnp.where(c, 1.0, 0.0) for c in chosen], axis=0)
    gate_ref[...] = jnp.concatenate(
        [jnp.where(chosen[e], gates[e : e + 1, :], 0.0) for e in range(experts)], axis=0
    )
    one_hot = one_hot.astype(jnp.bfloat16)
    for h in range(0, heads * width, 512):
        buf_ref[:, h : h + 512] = jnp.dot(
            one_hot, normed[:, h : h + 512], preferred_element_type=jnp.float32
        ).astype(jnp.bfloat16)


def route(residual, heads, router, routes, capacity):
    tokens, width = residual.shape
    experts = router.shape[0]
    slots = experts * SLOTS
    return pl.pallas_call(
        route_kernel,
        out_shape=(
            jax.ShapeDtypeStruct((slots, width), jnp.bfloat16),
            jax.ShapeDtypeStruct((slots, tokens), jnp.float32),
        ),
        scratch_shapes=[pltpu.VMEM((tokens, width), jnp.bfloat16)],
        compiler_params=pltpu.CompilerParams(vmem_limit_bytes=48 * MIB),
        name="route",
    )(residual, heads, router, routes, capacity)


def expert_kernel(x_ref, gate_own, up_own, down_own, gate_ref, up_ref, down_ref, o_ref, acc):
    group = pl.program_id(0)
    width = x_ref.shape[1]

    def contribute(gate_w, up_w, down_w, begin):
        x = x_ref[...]
        gate_out = jnp.dot(x, gate_w[...], preferred_element_type=jnp.float32)
        up_out = jnp.dot(x, up_w[...], preferred_element_type=jnp.float32)
        hidden = (gate_out / (1.0 + jnp.exp(-gate_out)) * up_out).astype(jnp.bfloat16)
        for c in range(0, width, 512):
            part = lax.dot_general(
                hidden, down_w[c : c + 512, :], contract_last, preferred_element_type=jnp.float32
            ).astype(jnp.bfloat16).astype(jnp.float32)
            if begin:
                acc[:, c : c + 512] = part
            else:
                acc[:, c : c + 512] += part

    @pl.when(group == 0)
    def _():
        contribute(gate_own, up_own, down_own, True)

    @pl.when(group > 0)
    def _():
        contribute(gate_ref, up_ref, down_ref, False)

    @pl.when(group == pl.num_programs(0) - 1)
    def _():
        o_ref[...] = acc[...].astype(o_ref.dtype)


def expert(x, own, others):
    rows, width = x.shape
    groups, _, hidden = others[0].shape
    groups += 1
    whole = pl.BlockSpec((width, hidden), lambda g: (0, 0), pipeline_mode=pl.Buffered(1))
    weight = pl.BlockSpec((None, width, hidden), lambda g: (jnp.maximum(g - 1, 0), 0, 0))
    return pl.pallas_call(
        expert_kernel,
        grid=(groups,),
        out_shape=jax.ShapeDtypeStruct((rows, width), jnp.bfloat16),
        in_specs=[pl.BlockSpec((rows, width), lambda g: (0, 0))] + [whole] * 3 + [weight] * 3,
        out_specs=pl.BlockSpec((rows, width), lambda g: (0, 0)),
        scratch_shapes=[pltpu.VMEM((rows, width), jnp.float32)],
        compiler_params=pltpu.CompilerParams(vmem_limit_bytes=56 * MIB),
        name="experts",
    )(x, *own, *others)


def combine_kernel(res_ref, heads_ref, back_ref, gate_ref, o_ref):
    heads = heads_ref.shape[0]
    gates = gate_ref[...]
    hi = gates.astype(jnp.bfloat16)
    lo = (gates - hi.astype(jnp.float32)).astype(jnp.bfloat16)
    for h in range(heads):
        columns = slice(h * LANES, (h + 1) * LANES)
        back = back_ref[:, columns]
        total = lax.dot_general(hi, back, contract_first, preferred_element_type=jnp.float32)
        total += lax.dot_general(lo, back, contract_first, preferred_element_type=jnp.float32)
        o_ref[:, columns] = (attend_columns(res_ref, heads_ref, h) + total).astype(o_ref.dtype)


def combine(residual, heads, back, gates):
    return pl.pallas_call(
        combine_kernel,
        out_shape=jax.ShapeDtypeStruct(residual.shape, jnp.bfloat16),
        compiler_params=pltpu.CompilerParams(vmem_limit_bytes=48 * MIB),
        name="combine",
    )(residual, heads, back, gates)


def shards(
    queries, key_rows, value_rows, residual, lambdas, router, gate_proj, up_proj, down_proj, routes, capacity
):
    tokens, width = queries.shape
    experts = router.shape[1]
    own = (gate_proj[0], up_proj[0], down_proj[0])
    mixed, *others = front(lambdas, queries, key_rows, value_rows, *own)

    buffer, gates = route(residual, mixed, router.T, routes.T, capacity.T)
    buffer = lax.all_to_all(
        buffer.reshape(experts, SLOTS, width), "ctx", split_axis=0, concat_axis=0, tiled=True
    )
    results = expert(buffer.reshape(experts * SLOTS, width), own, others)
    back = lax.all_to_all(
        results.reshape(experts, SLOTS, width), "ctx", split_axis=0, concat_axis=0, tiled=True
    )
    return combine(residual, mixed, back.reshape(experts * SLOTS, width), gates)


def solution(mesh):
    rows = P(("dp", "ctx", "exp"), None)
    weights = P("ctx", None, "exp")
    placed = (rows, rows, rows, rows, P(), P(), weights, weights, weights, rows, rows)
    return jax.shard_map(shards, mesh=mesh, in_specs=placed, out_specs=rows, check_vma=False)
```

```python
import functools
import math

import jax
import jax.numpy as jnp
from jax import lax
from jax.experimental import pallas as pl
from jax.experimental.pallas import tpu as pltpu
from jax.sharding import PartitionSpec as P

EPSILON = 1e-05
OUT_SCALE = 0.8
LOG2E = math.log2(math.e)
LOW = -1e30
LANES = 128
SLOTS = 40
ROOM = 48
MIB = 1024 * 1024
MESH = pl.DeviceIdType.MESH
contract_last = (((1,), (1,)), ((), ()))
contract_first = (((0,), (0,)), ((), ()))


def relative(ctx=0, exp=0, dp=0):
    def place(axis, step):
        size = lax.axis_size(axis)
        return lax.rem(lax.axis_index(axis) + step + size, size)

    return {"dp": place("dp", dp), "ctx": place("ctx", ctx), "exp": place("exp", exp)}


def attend_columns(res_ref, heads_ref, h):
    columns = slice(h * LANES, (h + 1) * LANES)
    return res_ref[:, columns].astype(jnp.float32) + heads_ref[h].astype(jnp.float32)


PARTS = 8
AHEAD = 4


def front_kernel(
    bq, bk, lam_ref, q_ref, k_ref, v_ref, gate_ref, up_ref, down_ref, res_ref, router_ref, routes_ref, cap_ref,
    heads_ref, gates_ref, x_ref, w_ref,
    qkv, mixed, kk, vv, qq, acc, largest, normed, buf,
    qkv_send, qkv_recv, out_send, out_recv, x_send, x_recv, w_send, far_recv, w_recv,
):
    _, sources, rows, width = qkv.shape
    length = sources * rows
    half = width // 2
    experts = buf.shape[0]
    fan = lax.axis_size("exp")
    me = lax.axis_index("ctx") * fan + lax.axis_index("exp")
    parity = lax.rem(lax.axis_index("dp"), 2)

    def member(index):
        return {"dp": lax.axis_index("dp"), "ctx": lax.div(index, fan), "exp": lax.rem(index, fan)}

    barrier = pltpu.get_barrier_semaphore()

    def greet(step, carried):
        pl.semaphore_signal(
            barrier, inc=1, device_id=member(lax.rem(me + step, sources)), device_id_type=MESH
        )
        return carried

    lax.fori_loop(1, sources, greet, 0)
    pl.semaphore_signal(barrier, inc=1, device_id=relative(dp=1), device_id_type=MESH)
    pl.semaphore_signal(barrier, inc=1, device_id=relative(dp=-1), device_id_type=MESH)
    pl.semaphore_wait(barrier, sources + 1)

    inputs = (q_ref, k_ref, v_ref)

    def send_heads(step, carried):
        target = lax.rem(me + step, sources)
        columns = pl.ds(pl.multiple_of(target * width, width), width)
        for which in range(3):
            pltpu.make_async_remote_copy(
                src_ref=inputs[which].at[:, columns],
                dst_ref=qkv.at[which, me],
                send_sem=qkv_send,
                recv_sem=qkv_recv,
                device_id=member(target),
                device_id_type=MESH,
            ).start()
        return carried

    lax.fori_loop(1, sources, send_heads, 0)
    own = pl.ds(pl.multiple_of(me * width, width), width)
    for which in range(3):
        pltpu.make_async_copy(inputs[which].at[:, own], qkv.at[which, me], qkv_recv).start()

    weights = (gate_ref, up_ref, down_ref)
    size = gate_ref.shape[0] // (2 * PARTS)
    total = len(weights) * PARTS

    def rows_of(part):
        return pl.ds(pl.multiple_of((parity * PARTS + part) * size, size), size)

    def push(src, array, slot, part, recv, device):
        pltpu.make_async_remote_copy(
            src_ref=src,
            dst_ref=w_ref.at[array * 3 + slot, rows_of(part)],
            send_sem=w_send,
            recv_sem=recv,
            device_id=device,
            device_id_type=MESH,
        ).start()

    def near(array, slot, part):
        return w_recv.at[(array * 3 + slot) * PARTS + part]

    def arrived(array, slot, part):
        block = w_ref.at[array * 3 + slot, rows_of(part)]
        pltpu.make_async_copy(block, block, near(array, slot, part)).wait()

    def first(k):
        part = lax.rem(k, PARTS)
        for array in range(len(weights)):

            @pl.when(lax.div(k, PARTS) == array)
            def _():
                for slot, step in ((1, 1), (0, -1)):
                    push(
                        weights[array].at[rows_of(part)], array, slot, part,
                        near(array, slot, part), relative(exp=step),
                    )

    def along(array, slot, part):
        push(
            w_ref.at[array * 3 + slot, rows_of(part)], array, slot, part, far_recv,
            relative(dp=1 - 2 * lax.rem(part, 2)),
        )

    def third(k):
        array, part = lax.div(k, PARTS), lax.rem(k, PARTS)
        arrived(array, 2, part)
        along(array, 2, part)

    def event(k, carried):
        array, part = lax.div(k, PARTS), lax.rem(k, PARTS)

        @pl.when(k + AHEAD < total)
        def _():
            first(k + AHEAD)

        odd = lax.rem(part, 2)
        arrived(array, 0, part)
        arrived(array, 1, part)
        slot = 1 - odd
        push(
            w_ref.at[array * 3 + slot, rows_of(part)], array, 2, part,
            near(array, 2, part), relative(exp=1 - 2 * odd),
        )
        along(array, 0, part)
        along(array, 1, part)

        @pl.when(k >= 1)
        def _():
            third(k - 1)

        return carried

    def begin(k, carried):
        first(k)
        return carried

    lax.fori_loop(0, AHEAD, begin, 0)
    lax.fori_loop(0, 4, event, 0)

    pltpu.make_async_copy(qkv, qkv, qkv_recv).wait()
    keys = qkv[1].reshape(length, width)
    kk[:, :width] = keys
    kk[:, width:] = keys
    vv[:, :width] = qkv[2].reshape(length, width)
    vv[:, width:] = jnp.ones((length, width), vv.dtype)

    per = bq // rows
    lam = lam_ref[me]

    def query_block(i, carried):
        lax.fori_loop(4 + i + lax.div(i, 3), 5 + i + lax.div(i, 2), event, 0)
        q = qkv[0, pl.ds(i * per, per)].reshape(bq, width)
        q = q.astype(jnp.float32) * (LOG2E / math.sqrt(half))
        hi = q.astype(jnp.bfloat16)
        lo = (q - hi.astype(jnp.float32)).astype(jnp.bfloat16)
        lower = lax.broadcasted_iota(jnp.int32, (bq, width), 1) < half
        zero = jnp.zeros((bq, width), jnp.bfloat16)
        qq[:bq, :width] = jnp.where(lower, hi, zero)
        qq[:bq, width:] = jnp.where(lower, lo, zero)
        qq[bq:, :width] = jnp.where(lower, zero, hi)
        qq[bq:, width:] = jnp.where(lower, zero, lo)
        acc[...] = jnp.zeros_like(acc)
        largest[...] = jnp.full_like(largest, LOW)

        def scores(j, masked):
            keys_here = pl.ds(pl.multiple_of(j * bk, bk), bk)
            s = lax.dot_general(
                qq[...], kk[keys_here, :], contract_last, preferred_element_type=jnp.float32
            )
            if masked:
                row = i * bq + lax.broadcasted_iota(jnp.int32, (bq, bk), 0)
                col = j * bk + lax.broadcasted_iota(jnp.int32, (bq, bk), 1)
                allowed = col <= row
                s = jnp.where(jnp.concatenate([allowed, allowed], axis=0), s, LOW)
            return s

        def look(j, masked):
            s = scores(j, masked)
            top = largest[...]
            for c in range(0, bk, width):
                top = jnp.maximum(top, s[:, c : c + width])
            largest[...] = top

        def add(j, masked):
            s = scores(j, masked)
            top = largest[...]
            raised = jnp.concatenate(
                [jnp.exp2(s[:, c : c + width] - top).astype(jnp.bfloat16) for c in range(0, bk, width)],
                axis=1,
            )
            keys_here = pl.ds(pl.multiple_of(j * bk, bk), bk)
            acc[...] += jnp.dot(raised, vv[keys_here, :], preferred_element_type=jnp.float32)

        full = lax.div(i * bq, bk)

        def look_body(j, inner):
            look(j, False)
            return inner

        def add_body(j, inner):
            add(j, False)
            return inner

        lax.fori_loop(0, full, look_body, 0)
        look(full, True)
        largest[...] = jnp.broadcast_to(
            jnp.max(largest[...], axis=1, keepdims=True), largest.shape
        )
        lax.fori_loop(0, full, add_body, 0)
        add(full, True)
        one = acc[:bq, :width] / acc[:bq, width:]
        two = acc[bq:, :width] / acc[bq:, width:]
        blend = one - lam * two
        mean = jnp.mean(blend * blend, axis=1, keepdims=True)
        out = (OUT_SCALE * blend * lax.rsqrt(mean + EPSILON)).astype(mixed.dtype)
        mixed[pl.ds(i * per, per)] = out.reshape(per, rows, width)

        def send_rows(r, inner):
            target = i * per + r

            @pl.when(target != me)
            def _():
                pltpu.make_async_remote_copy(
                    src_ref=mixed.at[target],
                    dst_ref=heads_ref.at[me],
                    send_sem=out_send,
                    recv_sem=out_recv,
                    device_id=member(target),
                    device_id_type=MESH,
                ).start()

            @pl.when(target == me)
            def _():
                pltpu.make_async_copy(mixed.at[target], heads_ref.at[me], out_recv).start()

            return inner

        lax.fori_loop(0, per, send_rows, 0)
        return carried

    blocks = length // bq
    lax.fori_loop(0, blocks, query_block, 0)
    pltpu.make_async_copy(heads_ref, heads_ref, out_recv).wait()
    route(res_ref, heads_ref, router_ref, routes_ref, cap_ref, gates_ref, normed, buf)

    here = lax.axis_index("ctx")

    def send_expert(step, carried):
        target = lax.rem(here + step, experts)
        pltpu.make_async_remote_copy(
            src_ref=buf.at[target],
            dst_ref=x_ref.at[here],
            send_sem=x_send,
            recv_sem=x_recv,
            device_id=relative(ctx=step),
            device_id_type=MESH,
        ).start()
        return carried

    lax.fori_loop(1, experts, send_expert, 0)
    pltpu.make_async_copy(buf.at[here], x_ref.at[here], x_recv).start()

    lax.fori_loop(4 + blocks + lax.div(blocks, 3), total, event, 0)
    third(total - 1)
    others = pl.ds(0, sources - 1)
    for which in range(3):
        pltpu.make_async_copy(qkv.at[which, others], qkv.at[which, others], qkv_send).wait()
    pltpu.make_async_copy(mixed.at[others], mixed.at[others], out_send).wait()
    pltpu.make_async_copy(buf.at[pl.ds(1, experts - 1)], buf.at[pl.ds(1, experts - 1)], x_send).wait()
    pltpu.make_async_copy(x_ref, x_ref, x_recv).wait()
    halves = size * PARTS
    far = w_ref.at[:, pl.ds(pl.multiple_of((1 - parity) * halves, halves), halves)]
    pltpu.make_async_copy(far, far, far_recv).wait()
    pltpu.make_async_copy(w_ref, w_ref, w_send).wait()


def route(res_ref, heads_ref, router_ref, routes_ref, cap_ref, gates_ref, normed, buf):
    heads, tokens, width = heads_ref.shape
    experts, room, _ = buf.shape
    square = jnp.zeros((tokens, width), jnp.float32)
    for h in range(heads):
        block = attend_columns(res_ref, heads_ref, h)
        square = square + block * block
    mean = jnp.sum(square, axis=1, keepdims=True) / (heads * width)
    factor = lax.rsqrt(mean + EPSILON)
    for h in range(heads):
        block = attend_columns(res_ref, heads_ref, h)
        normed[:, h * width : (h + 1) * width] = (block * factor).astype(jnp.bfloat16)
    logits = lax.dot_general(
        router_ref[...], normed[...], contract_last, preferred_element_type=jnp.float32
    )
    sig = 1.0 / (1.0 + jnp.exp(-logits))
    expert_of = lax.broadcasted_iota(jnp.int32, (experts, tokens), 0)
    named = (routes_ref[0:1, :] == expert_of) | (routes_ref[1:2, :] == expert_of)
    picked = jnp.where(named, sig, 0.0)
    gates = picked / jnp.sum(picked, axis=0, keepdims=True)
    before = lax.broadcasted_iota(jnp.int32, (tokens, tokens), 0) < lax.broadcasted_iota(
        jnp.int32, (tokens, tokens), 1
    )
    position = jnp.dot(
        jnp.where(named, 1.0, 0.0).astype(jnp.bfloat16),
        jnp.where(before, 1.0, 0.0).astype(jnp.bfloat16),
        preferred_element_type=jnp.float32,
    )
    kept = named & (position < cap_ref[...].astype(jnp.float32))
    position = jnp.where(kept, position, -1.0).astype(jnp.int32)
    slot = lax.broadcasted_iota(jnp.int32, (room, tokens), 0)
    chosen = [slot == position[e : e + 1, :] for e in range(experts)]
    one_hot = jnp.concatenate([jnp.where(c, 1.0, 0.0) for c in chosen], axis=0).astype(jnp.bfloat16)
    gates_ref[...] = jnp.concatenate(
        [jnp.where(chosen[e][:SLOTS], gates[e : e + 1, :], 0.0) for e in range(experts)], axis=0
    )
    for column in range(0, heads * width, 512):
        columns = slice(column, column + 512)
        moved = jnp.dot(one_hot, normed[:, columns], preferred_element_type=jnp.float32)
        buf[:, :, columns] = moved.astype(jnp.bfloat16).reshape(experts, room, 512)


def front(lambdas, queries, key_rows, value_rows, own, residual, router, routes, capacity, bq=1024, bk=1024):
    rows, total = queries.shape
    experts = router.shape[0]
    width = LANES
    heads = total // width
    length = heads * rows
    anywhere = pl.BlockSpec(memory_space=pl.ANY)
    vmem = pl.BlockSpec(memory_space=pltpu.VMEM)
    slots = len(own) * (lax.axis_size("exp") - 1)
    dma = pltpu.SemaphoreType.DMA
    return pl.pallas_call(
        functools.partial(front_kernel, bq, bk),
        out_shape=(
            jax.ShapeDtypeStruct((heads, rows, width), jnp.bfloat16),
            jax.ShapeDtypeStruct((experts * SLOTS, rows), jnp.float32),
            jax.ShapeDtypeStruct((experts, ROOM, total), jnp.bfloat16),
            jax.ShapeDtypeStruct((slots, *own[0].shape), jnp.bfloat16),
        ),
        in_specs=[pl.BlockSpec(memory_space=pltpu.SMEM)] + [anywhere] * 6 + [vmem] * 4,
        out_specs=(vmem, vmem, anywhere, anywhere),
        scratch_shapes=[
            pltpu.VMEM((3, heads, rows, width), jnp.bfloat16),
            pltpu.VMEM((heads, rows, width), jnp.bfloat16),
            pltpu.VMEM((length, 2 * width), jnp.bfloat16),
            pltpu.VMEM((length, 2 * width), jnp.bfloat16),
            pltpu.VMEM((2 * bq, 2 * width), jnp.bfloat16),
            pltpu.VMEM((2 * bq, 2 * width), jnp.float32),
            pltpu.VMEM((2 * bq, width), jnp.float32),
            pltpu.VMEM((rows, total), jnp.bfloat16),
            pltpu.VMEM((experts, ROOM, total), jnp.bfloat16),
        ]
        + [dma] * 8
        + [dma((slots * PARTS,))],
        compiler_params=pltpu.CompilerParams(
            vmem_limit_bytes=58 * MIB, collective_id=0, has_side_effects=True
        ),
        name="front",
    )(lambdas, queries, key_rows, value_rows, *own, residual, router, routes, capacity)


def expert_kernel(x_ref, gate_own, up_own, down_own, gate_ref, up_ref, down_ref, o_ref, x_all, acc):
    group = pl.program_id(0)
    sources, _, width = x_ref.shape

    def contribute(gate_w, up_w, down_w, begin):
        x = x_all[...]
        gate_out = jnp.dot(x, gate_w[...], preferred_element_type=jnp.float32)
        up_out = jnp.dot(x, up_w[...], preferred_element_type=jnp.float32)
        hidden = (gate_out / (1.0 + jnp.exp(-gate_out)) * up_out).astype(jnp.bfloat16)
        for c in range(0, width, 512):
            part = lax.dot_general(
                hidden, down_w[c : c + 512, :], contract_last, preferred_element_type=jnp.float32
            ).astype(jnp.bfloat16).astype(jnp.float32)
            if begin:
                acc[:, c : c + 512] = part
            else:
                acc[:, c : c + 512] += part

    @pl.when(group == 0)
    def _():
        for c in range(0, width, 512):
            parts = [
                x_ref[s, :, c : c + 512].astype(jnp.float32)[:SLOTS] for s in range(sources)
            ]
            x_all[:, c : c + 512] = jnp.concatenate(parts, axis=0).astype(x_all.dtype)
        contribute(gate_own, up_own, down_own, True)

    @pl.when(group > 0)
    def _():
        contribute(gate_ref, up_ref, down_ref, False)

    @pl.when(group == pl.num_programs(0) - 1)
    def _():
        o_ref[...] = acc[...].astype(o_ref.dtype)


def expert(x, own, others):
    sources, room, width = x.shape
    rows = sources * SLOTS
    slots, _, hidden = others.shape
    arrays = len(own)
    each = slots // arrays
    whole = pl.BlockSpec((width, hidden), lambda g: (0, 0), pipeline_mode=pl.Buffered(1))

    def weight(array):
        return pl.BlockSpec(
            (None, width, hidden), lambda g: (array * each + jnp.maximum(g - 1, 0), 0, 0)
        )

    return pl.pallas_call(
        expert_kernel,
        grid=(each + 1,),
        out_shape=jax.ShapeDtypeStruct((rows, width), jnp.bfloat16),
        in_specs=[pl.BlockSpec((sources, room, width), lambda g: (0, 0, 0), pipeline_mode=pl.Buffered(1))]
        + [whole] * arrays
        + [weight(a) for a in range(arrays)],
        out_specs=pl.BlockSpec((rows, width), lambda g: (0, 0)),
        scratch_shapes=[pltpu.VMEM((rows, width), jnp.bfloat16), pltpu.VMEM((rows, width), jnp.float32)],
        compiler_params=pltpu.CompilerParams(vmem_limit_bytes=56 * MIB),
        name="experts",
    )(x, *own, others, others, others)


def combine_kernel(res_ref, heads_ref, back_ref, gate_ref, o_ref):
    heads = heads_ref.shape[0]
    gates = gate_ref[...]
    hi = gates.astype(jnp.bfloat16)
    lo = (gates - hi.astype(jnp.float32)).astype(jnp.bfloat16)
    for h in range(heads):
        columns = slice(h * LANES, (h + 1) * LANES)
        back = back_ref[:, columns]
        total = lax.dot_general(hi, back, contract_first, preferred_element_type=jnp.float32)
        total += lax.dot_general(lo, back, contract_first, preferred_element_type=jnp.float32)
        o_ref[:, columns] = (attend_columns(res_ref, heads_ref, h) + total).astype(o_ref.dtype)


def combine(residual, heads, back, gates):
    return pl.pallas_call(
        combine_kernel,
        out_shape=jax.ShapeDtypeStruct(residual.shape, jnp.bfloat16),
        compiler_params=pltpu.CompilerParams(vmem_limit_bytes=48 * MIB),
        name="combine",
    )(residual, heads, back, gates)


def shards(
    queries, key_rows, value_rows, residual, lambdas, router, gate_proj, up_proj, down_proj, routes, capacity
):
    tokens, width = queries.shape
    experts = router.shape[1]
    own = (gate_proj[0], up_proj[0], down_proj[0])
    mixed, gates, x, others = front(
        lambdas, queries, key_rows, value_rows, own, residual, router.T, routes.T, capacity.T
    )
    results = expert(x, own, others)
    back = lax.all_to_all(
        results.reshape(experts, SLOTS, width), "ctx", split_axis=0, concat_axis=0, tiled=True
    )
    return combine(residual, mixed, back.reshape(experts * SLOTS, width), gates)


def solution(mesh):
    rows = P(("dp", "ctx", "exp"), None)
    weights = P("ctx", None, "exp")
    placed = (rows, rows, rows, rows, P(), P(), weights, weights, weights, rows, rows)
    return jax.shard_map(shards, mesh=mesh, in_specs=placed, out_specs=rows, check_vma=False)
```

```python
import functools
import math

import jax
import jax.numpy as jnp
from jax import lax
from jax.experimental import pallas as pl
from jax.experimental.pallas import tpu as pltpu
from jax.sharding import PartitionSpec as P

EPSILON = 1e-05
OUT_SCALE = 0.8
LOG2E = math.log2(math.e)
LOW = -1e30
LANES = 128
SLOTS = 40
ROOM = 48
MIB = 1024 * 1024
MESH = pl.DeviceIdType.MESH
contract_last = (((1,), (1,)), ((), ()))
contract_first = (((0,), (0,)), ((), ()))


def relative(ctx=0, exp=0, dp=0):
    def place(axis, step):
        size = lax.axis_size(axis)
        return lax.rem(lax.axis_index(axis) + step + size, size)

    return {"dp": place("dp", dp), "ctx": place("ctx", ctx), "exp": place("exp", exp)}


def attend_columns(res_ref, heads_ref, h):
    columns = slice(h * LANES, (h + 1) * LANES)
    return res_ref[:, columns].astype(jnp.float32) + heads_ref[h].astype(jnp.float32)


PARTS = 8
EARLY = 3
AHEAD = 3


def front_kernel(
    bq, bk, lam_ref, q_ref, k_ref, v_ref, gate_ref, up_ref, down_ref, res_ref, router_ref, routes_ref, cap_ref,
    heads_ref, gates_ref, x_ref, w_ref,
    qkv, mixed, kk, vv, qq, acc, largest, normed, buf,
    qkv_send, qkv_recv, out_send, out_recv, x_send, x_recv, w_send, far_recv, w_recv,
):
    _, sources, rows, width = qkv.shape
    length = sources * rows
    half = width // 2
    experts = buf.shape[0]
    fan = lax.axis_size("exp")
    me = lax.axis_index("ctx") * fan + lax.axis_index("exp")
    parity = lax.rem(lax.axis_index("dp"), 2)

    def member(index):
        return {"dp": lax.axis_index("dp"), "ctx": lax.div(index, fan), "exp": lax.rem(index, fan)}

    barrier = pltpu.get_barrier_semaphore()

    def greet(step, carried):
        pl.semaphore_signal(
            barrier, inc=1, device_id=member(lax.rem(me + step, sources)), device_id_type=MESH
        )
        return carried

    lax.fori_loop(1, sources, greet, 0)
    pl.semaphore_signal(barrier, inc=1, device_id=relative(dp=1), device_id_type=MESH)
    pl.semaphore_signal(barrier, inc=1, device_id=relative(dp=-1), device_id_type=MESH)
    pl.semaphore_wait(barrier, sources + 1)

    inputs = (q_ref, k_ref, v_ref)

    def send_heads(step, carried):
        target = lax.rem(me + step, sources)
        columns = pl.ds(pl.multiple_of(target * width, width), width)
        for which in range(3):
            pltpu.make_async_remote_copy(
                src_ref=inputs[which].at[:, columns],
                dst_ref=qkv.at[which, me],
                send_sem=qkv_send,
                recv_sem=qkv_recv,
                device_id=member(target),
                device_id_type=MESH,
            ).start()
        return carried

    lax.fori_loop(1, sources, send_heads, 0)
    own = pl.ds(pl.multiple_of(me * width, width), width)
    for which in range(3):
        pltpu.make_async_copy(inputs[which].at[:, own], qkv.at[which, me], qkv_recv).start()

    weights = (gate_ref, up_ref, down_ref)
    size = gate_ref.shape[0] // (2 * PARTS)
    total = len(weights) * PARTS

    def rows_of(part):
        return pl.ds(pl.multiple_of((parity * PARTS + part) * size, size), size)

    def push(src, array, slot, part, recv, device):
        pltpu.make_async_remote_copy(
            src_ref=src,
            dst_ref=w_ref.at[array * 3 + slot, rows_of(part)],
            send_sem=w_send,
            recv_sem=recv,
            device_id=device,
            device_id_type=MESH,
        ).start()

    def near(array, slot, part):
        return w_recv.at[(array * 3 + slot) * PARTS + part]

    def arrived(array, slot, part):
        block = w_ref.at[array * 3 + slot, rows_of(part)]
        pltpu.make_async_copy(block, block, near(array, slot, part)).wait()

    def first(k):
        part = lax.rem(k, PARTS)
        for array in range(len(weights)):

            @pl.when(lax.div(k, PARTS) == array)
            def _():
                for slot, step in ((1, 1), (0, -1)):
                    push(
                        weights[array].at[rows_of(part)], array, slot, part,
                        near(array, slot, part), relative(exp=step),
                    )

    def along(array, slot, part):
        push(
            w_ref.at[array * 3 + slot, rows_of(part)], array, slot, part, far_recv,
            relative(dp=1 - 2 * lax.rem(part, 2)),
        )

    def third(k):
        array, part = lax.div(k, PARTS), lax.rem(k, PARTS)
        arrived(array, 2, part)
        along(array, 2, part)

    def event(k, carried):
        array, part = lax.div(k, PARTS), lax.rem(k, PARTS)

        @pl.when(k + AHEAD < total)
        def _():
            first(k + AHEAD)

        odd = lax.rem(part, 2)
        arrived(array, 0, part)
        arrived(array, 1, part)
        slot = 1 - odd
        push(
            w_ref.at[array * 3 + slot, rows_of(part)], array, 2, part,
            near(array, 2, part), relative(exp=1 - 2 * odd),
        )
        along(array, 0, part)
        along(array, 1, part)

        @pl.when(k >= 2)
        def _():
            third(k - 2)

        return carried

    def begin(k, carried):
        first(k)
        return carried

    lax.fori_loop(0, AHEAD, begin, 0)
    lax.fori_loop(0, EARLY, event, 0)

    pltpu.make_async_copy(qkv, qkv, qkv_recv).wait()
    keys = qkv[1].reshape(length, width)
    kk[:, :width] = keys
    kk[:, width:] = keys
    vv[:, :width] = qkv[2].reshape(length, width)
    vv[:, width:] = jnp.ones((length, width), vv.dtype)

    per = bq // rows
    lam = lam_ref[me]

    blocks = length // bq
    start = lax.rem(lax.axis_index("ctx"), blocks)
    chunks = blocks * (blocks + 1) // 2

    def query_block(turn, carried):
        i = lax.rem(start + turn, blocks)
        done = EARLY + chunks * lax.div(start + turn, blocks)
        done = done + lax.div(i * (i + 1), 2) - lax.div(start * (start + 1), 2)

        def weight_step(j, phase):
            @pl.when(lax.rem(j, 2) == phase)
            def _():
                event(done + lax.div(j, 2) + phase * (lax.div(i, 2) + 1), 0)

        q = qkv[0, pl.ds(i * per, per)].reshape(bq, width)
        q = q.astype(jnp.float32) * (LOG2E / math.sqrt(half))
        hi = q.astype(jnp.bfloat16)
        lo = (q - hi.astype(jnp.float32)).astype(jnp.bfloat16)
        lower = lax.broadcasted_iota(jnp.int32, (bq, width), 1) < half
        zero = jnp.zeros((bq, width), jnp.bfloat16)
        qq[:bq, :width] = jnp.where(lower, hi, zero)
        qq[:bq, width:] = jnp.where(lower, lo, zero)
        qq[bq:, :width] = jnp.where(lower, zero, hi)
        qq[bq:, width:] = jnp.where(lower, zero, lo)
        acc[...] = jnp.zeros_like(acc)
        largest[...] = jnp.full_like(largest, LOW)

        def scores(j, masked):
            keys_here = pl.ds(pl.multiple_of(j * bk, bk), bk)
            s = lax.dot_general(
                qq[...], kk[keys_here, :], contract_last, preferred_element_type=jnp.float32
            )
            if masked:
                row = i * bq + lax.broadcasted_iota(jnp.int32, (bq, bk), 0)
                col = j * bk + lax.broadcasted_iota(jnp.int32, (bq, bk), 1)
                allowed = col <= row
                s = jnp.where(jnp.concatenate([allowed, allowed], axis=0), s, LOW)
            return s

        def look(j, masked):
            weight_step(j, 0)
            s = scores(j, masked)
            top = largest[...]
            for c in range(0, bk, width):
                top = jnp.maximum(top, s[:, c : c + width])
            largest[...] = top

        def add(j, masked):
            weight_step(j, 1)
            s = scores(j, masked)
            top = largest[...]
            raised = jnp.concatenate(
                [jnp.exp2(s[:, c : c + width] - top).astype(jnp.bfloat16) for c in range(0, bk, width)],
                axis=1,
            )
            keys_here = pl.ds(pl.multiple_of(j * bk, bk), bk)
            acc[...] += jnp.dot(raised, vv[keys_here, :], preferred_element_type=jnp.float32)

        full = lax.div(i * bq, bk)

        def look_body(j, inner):
            look(j, False)
            return inner

        def add_body(j, inner):
            add(j, False)
            return inner

        lax.fori_loop(0, full, look_body, 0)
        look(full, True)
        largest[...] = jnp.broadcast_to(
            jnp.max(largest[...], axis=1, keepdims=True), largest.shape
        )
        lax.fori_loop(0, full, add_body, 0)
        add(full, True)
        one = acc[:bq, :width] / acc[:bq, width:]
        two = acc[bq:, :width] / acc[bq:, width:]
        blend = one - lam * two
        mean = jnp.mean(blend * blend, axis=1, keepdims=True)
        out = (OUT_SCALE * blend * lax.rsqrt(mean + EPSILON)).astype(mixed.dtype)
        mixed[pl.ds(i * per, per)] = out.reshape(per, rows, width)

        def send_rows(r, inner):
            target = i * per + r

            @pl.when(target != me)
            def _():
                pltpu.make_async_remote_copy(
                    src_ref=mixed.at[target],
                    dst_ref=heads_ref.at[me],
                    send_sem=out_send,
                    recv_sem=out_recv,
                    device_id=member(target),
                    device_id_type=MESH,
                ).start()

            @pl.when(target == me)
            def _():
                pltpu.make_async_copy(mixed.at[target], heads_ref.at[me], out_recv).start()

            return inner

        lax.fori_loop(0, per, send_rows, 0)
        return carried

    lax.fori_loop(0, blocks, query_block, 0)
    pltpu.make_async_copy(heads_ref, heads_ref, out_recv).wait()
    route(res_ref, heads_ref, router_ref, routes_ref, cap_ref, gates_ref, normed, buf)

    here = lax.axis_index("ctx")

    def send_expert(step, carried):
        target = lax.rem(here + step, experts)
        pltpu.make_async_remote_copy(
            src_ref=buf.at[target],
            dst_ref=x_ref.at[here],
            send_sem=x_send,
            recv_sem=x_recv,
            device_id=relative(ctx=step),
            device_id_type=MESH,
        ).start()
        return carried

    lax.fori_loop(1, experts, send_expert, 0)
    pltpu.make_async_copy(buf.at[here], x_ref.at[here], x_recv).start()

    lax.fori_loop(EARLY + chunks, total, event, 0)
    third(total - 2)
    third(total - 1)
    others = pl.ds(0, sources - 1)
    for which in range(3):
        pltpu.make_async_copy(qkv.at[which, others], qkv.at[which, others], qkv_send).wait()
    pltpu.make_async_copy(mixed.at[others], mixed.at[others], out_send).wait()
    pltpu.make_async_copy(buf.at[pl.ds(1, experts - 1)], buf.at[pl.ds(1, experts - 1)], x_send).wait()
    pltpu.make_async_copy(x_ref, x_ref, x_recv).wait()
    halves = size * PARTS
    far = w_ref.at[:, pl.ds(pl.multiple_of((1 - parity) * halves, halves), halves)]
    pltpu.make_async_copy(far, far, far_recv).wait()
    pltpu.make_async_copy(w_ref, w_ref, w_send).wait()


def route(res_ref, heads_ref, router_ref, routes_ref, cap_ref, gates_ref, normed, buf):
    heads, tokens, width = heads_ref.shape
    experts, room, _ = buf.shape
    square = jnp.zeros((tokens, width), jnp.float32)
    for h in range(heads):
        block = attend_columns(res_ref, heads_ref, h)
        square = square + block * block
    mean = jnp.sum(square, axis=1, keepdims=True) / (heads * width)
    factor = lax.rsqrt(mean + EPSILON)
    for h in range(heads):
        block = attend_columns(res_ref, heads_ref, h)
        normed[:, h * width : (h + 1) * width] = (block * factor).astype(jnp.bfloat16)
    logits = lax.dot_general(
        router_ref[...], normed[...], contract_last, preferred_element_type=jnp.float32
    )
    sig = 1.0 / (1.0 + jnp.exp(-logits))
    expert_of = lax.broadcasted_iota(jnp.int32, (experts, tokens), 0)
    named = (routes_ref[0:1, :] == expert_of) | (routes_ref[1:2, :] == expert_of)
    picked = jnp.where(named, sig, 0.0)
    gates = picked / jnp.sum(picked, axis=0, keepdims=True)
    before = lax.broadcasted_iota(jnp.int32, (tokens, tokens), 0) < lax.broadcasted_iota(
        jnp.int32, (tokens, tokens), 1
    )
    position = jnp.dot(
        jnp.where(named, 1.0, 0.0).astype(jnp.bfloat16),
        jnp.where(before, 1.0, 0.0).astype(jnp.bfloat16),
        preferred_element_type=jnp.float32,
    )
    kept = named & (position < cap_ref[...].astype(jnp.float32))
    position = jnp.where(kept, position, -1.0).astype(jnp.int32)
    slot = lax.broadcasted_iota(jnp.int32, (room, tokens), 0)
    chosen = [slot == position[e : e + 1, :] for e in range(experts)]
    one_hot = jnp.concatenate([jnp.where(c, 1.0, 0.0) for c in chosen], axis=0).astype(jnp.bfloat16)
    gates_ref[...] = jnp.concatenate(
        [jnp.where(chosen[e][:SLOTS], gates[e : e + 1, :], 0.0) for e in range(experts)], axis=0
    )
    for column in range(0, heads * width, 512):
        columns = slice(column, column + 512)
        moved = jnp.dot(one_hot, normed[:, columns], preferred_element_type=jnp.float32)
        buf[:, :, columns] = moved.astype(jnp.bfloat16).reshape(experts, room, 512)


def front(lambdas, queries, key_rows, value_rows, own, residual, router, routes, capacity, bq=1024, bk=1024):
    rows, total = queries.shape
    experts = router.shape[0]
    width = LANES
    heads = total // width
    length = heads * rows
    anywhere = pl.BlockSpec(memory_space=pl.ANY)
    vmem = pl.BlockSpec(memory_space=pltpu.VMEM)
    slots = len(own) * (lax.axis_size("exp") - 1)
    dma = pltpu.SemaphoreType.DMA
    return pl.pallas_call(
        functools.partial(front_kernel, bq, bk),
        out_shape=(
            jax.ShapeDtypeStruct((heads, rows, width), jnp.bfloat16),
            jax.ShapeDtypeStruct((experts * SLOTS, rows), jnp.float32),
            jax.ShapeDtypeStruct((experts, ROOM, total), jnp.bfloat16),
            jax.ShapeDtypeStruct((slots, *own[0].shape), jnp.bfloat16),
        ),
        in_specs=[pl.BlockSpec(memory_space=pltpu.SMEM)] + [anywhere] * 6 + [vmem] * 4,
        out_specs=(vmem, vmem, anywhere, anywhere),
        scratch_shapes=[
            pltpu.VMEM((3, heads, rows, width), jnp.bfloat16),
            pltpu.VMEM((heads, rows, width), jnp.bfloat16),
            pltpu.VMEM((length, 2 * width), jnp.bfloat16),
            pltpu.VMEM((length, 2 * width), jnp.bfloat16),
            pltpu.VMEM((2 * bq, 2 * width), jnp.bfloat16),
            pltpu.VMEM((2 * bq, 2 * width), jnp.float32),
            pltpu.VMEM((2 * bq, width), jnp.float32),
            pltpu.VMEM((rows, total), jnp.bfloat16),
            pltpu.VMEM((experts, ROOM, total), jnp.bfloat16),
        ]
        + [dma] * 8
        + [dma((slots * PARTS,))],
        compiler_params=pltpu.CompilerParams(
            vmem_limit_bytes=58 * MIB, collective_id=0, has_side_effects=True
        ),
        name="front",
    )(lambdas, queries, key_rows, value_rows, *own, residual, router, routes, capacity)


def expert_kernel(x_ref, gate_own, up_own, down_own, gate_ref, up_ref, down_ref, o_ref, x_all, acc):
    group = pl.program_id(0)
    sources, _, width = x_ref.shape

    def contribute(gate_w, up_w, down_w, begin):
        x = x_all[...]
        gate_out = jnp.dot(x, gate_w[...], preferred_element_type=jnp.float32)
        up_out = jnp.dot(x, up_w[...], preferred_element_type=jnp.float32)
        hidden = (gate_out / (1.0 + jnp.exp(-gate_out)) * up_out).astype(jnp.bfloat16)
        for c in range(0, width, 512):
            part = lax.dot_general(
                hidden, down_w[c : c + 512, :], contract_last, preferred_element_type=jnp.float32
            ).astype(jnp.bfloat16).astype(jnp.float32)
            if begin:
                acc[:, c : c + 512] = part
            else:
                acc[:, c : c + 512] += part

    @pl.when(group == 0)
    def _():
        for c in range(0, width, 512):
            parts = [
                x_ref[s, :, c : c + 512].astype(jnp.float32)[:SLOTS] for s in range(sources)
            ]
            x_all[:, c : c + 512] = jnp.concatenate(parts, axis=0).astype(x_all.dtype)
        contribute(gate_own, up_own, down_own, True)

    @pl.when(group > 0)
    def _():
        contribute(gate_ref, up_ref, down_ref, False)

    @pl.when(group == pl.num_programs(0) - 1)
    def _():
        o_ref[...] = acc[...].astype(o_ref.dtype)


def expert(x, own, others):
    sources, room, width = x.shape
    rows = sources * SLOTS
    slots, _, hidden = others.shape
    arrays = len(own)
    each = slots // arrays
    whole = pl.BlockSpec((width, hidden), lambda g: (0, 0), pipeline_mode=pl.Buffered(1))

    def weight(array):
        return pl.BlockSpec(
            (None, width, hidden), lambda g: (array * each + jnp.maximum(g - 1, 0), 0, 0)
        )

    return pl.pallas_call(
        expert_kernel,
        grid=(each + 1,),
        out_shape=jax.ShapeDtypeStruct((rows, width), jnp.bfloat16),
        in_specs=[pl.BlockSpec((sources, room, width), lambda g: (0, 0, 0), pipeline_mode=pl.Buffered(1))]
        + [whole] * arrays
        + [weight(a) for a in range(arrays)],
        out_specs=pl.BlockSpec((rows, width), lambda g: (0, 0)),
        scratch_shapes=[pltpu.VMEM((rows, width), jnp.bfloat16), pltpu.VMEM((rows, width), jnp.float32)],
        compiler_params=pltpu.CompilerParams(vmem_limit_bytes=56 * MIB),
        name="experts",
    )(x, *own, others, others, others)


def combine_kernel(res_ref, heads_ref, back_ref, gate_ref, o_ref):
    heads = heads_ref.shape[0]
    gates = gate_ref[...]
    hi = gates.astype(jnp.bfloat16)
    lo = (gates - hi.astype(jnp.float32)).astype(jnp.bfloat16)
    for h in range(heads):
        columns = slice(h * LANES, (h + 1) * LANES)
        back = back_ref[:, columns]
        total = lax.dot_general(hi, back, contract_first, preferred_element_type=jnp.float32)
        total += lax.dot_general(lo, back, contract_first, preferred_element_type=jnp.float32)
        o_ref[:, columns] = (attend_columns(res_ref, heads_ref, h) + total).astype(o_ref.dtype)


def combine(residual, heads, back, gates):
    return pl.pallas_call(
        combine_kernel,
        out_shape=jax.ShapeDtypeStruct(residual.shape, jnp.bfloat16),
        compiler_params=pltpu.CompilerParams(vmem_limit_bytes=48 * MIB),
        name="combine",
    )(residual, heads, back, gates)


def shards(
    queries, key_rows, value_rows, residual, lambdas, router, gate_proj, up_proj, down_proj, routes, capacity
):
    tokens, width = queries.shape
    experts = router.shape[1]
    own = (gate_proj[0], up_proj[0], down_proj[0])
    mixed, gates, x, others = front(
        lambdas, queries, key_rows, value_rows, own, residual, router.T, routes.T, capacity.T
    )
    results = expert(x, own, others)
    back = lax.all_to_all(
        results.reshape(experts, SLOTS, width), "ctx", split_axis=0, concat_axis=0, tiled=True
    )
    return combine(residual, mixed, back.reshape(experts * SLOTS, width), gates)


def solution(mesh):
    rows = P(("dp", "ctx", "exp"), None)
    weights = P("ctx", None, "exp")
    placed = (rows, rows, rows, rows, P(), P(), weights, weights, weights, rows, rows)
    return jax.shard_map(shards, mesh=mesh, in_specs=placed, out_specs=rows, check_vma=False)
```

```python
import functools
import math

import jax
import jax.numpy as jnp
from jax import lax
from jax.experimental import pallas as pl
from jax.experimental.pallas import tpu as pltpu
from jax.sharding import PartitionSpec as P

EPSILON = 1e-05
OUT_SCALE = 0.8
LOG2E = math.log2(math.e)
LOW = -1e30
LANES = 128
SLOTS = 40
ROOM = 48
MIB = 1024 * 1024
MESH = pl.DeviceIdType.MESH
contract_last = (((1,), (1,)), ((), ()))
contract_first = (((0,), (0,)), ((), ()))


def relative(ctx=0, exp=0, dp=0):
    def place(axis, step):
        size = lax.axis_size(axis)
        return lax.rem(lax.axis_index(axis) + step + size, size)

    return {"dp": place("dp", dp), "ctx": place("ctx", ctx), "exp": place("exp", exp)}


def attend_columns(res_ref, heads_ref, h):
    columns = slice(h * LANES, (h + 1) * LANES)
    return res_ref[:, columns].astype(jnp.float32) + heads_ref[h].astype(jnp.float32)


PARTS = 8
EARLY = 3
AHEAD = 3


def front_kernel(
    bq, bk, lam_ref, q_ref, k_ref, v_ref, gate_ref, up_ref, down_ref, res_ref, router_ref, routes_ref, cap_ref,
    heads_ref, gates_ref, x_ref, w_ref,
    qkv, mixed, kk, vv, qq, acc, largest, normed, buf,
    qkv_send, qkv_recv, out_send, out_recv, x_send, x_recv, w_send, far_recv, w_recv,
):
    _, sources, rows, width = qkv.shape
    length = sources * rows
    half = width // 2
    experts = buf.shape[0]
    fan = lax.axis_size("exp")
    me = lax.axis_index("ctx") * fan + lax.axis_index("exp")
    parity = lax.rem(lax.axis_index("dp"), 2)

    def member(index):
        return {"dp": lax.axis_index("dp"), "ctx": lax.div(index, fan), "exp": lax.rem(index, fan)}

    barrier = pltpu.get_barrier_semaphore()

    def greet(step, carried):
        pl.semaphore_signal(
            barrier, inc=1, device_id=member(lax.rem(me + step, sources)), device_id_type=MESH
        )
        return carried

    lax.fori_loop(1, sources, greet, 0)
    pl.semaphore_signal(barrier, inc=1, device_id=relative(dp=1), device_id_type=MESH)
    pl.semaphore_signal(barrier, inc=1, device_id=relative(dp=-1), device_id_type=MESH)
    pl.semaphore_wait(barrier, sources + 1)

    inputs = (q_ref, k_ref, v_ref)

    def send_heads(step, carried):
        target = lax.rem(me + step, sources)
        columns = pl.ds(pl.multiple_of(target * width, width), width)
        for which in range(3):
            pltpu.make_async_remote_copy(
                src_ref=inputs[which].at[:, columns],
                dst_ref=qkv.at[which, me],
                send_sem=qkv_send,
                recv_sem=qkv_recv,
                device_id=member(target),
                device_id_type=MESH,
            ).start()
        return carried

    lax.fori_loop(1, sources, send_heads, 0)
    own = pl.ds(pl.multiple_of(me * width, width), width)
    for which in range(3):
        pltpu.make_async_copy(inputs[which].at[:, own], qkv.at[which, me], qkv_recv).start()

    weights = (gate_ref, up_ref, down_ref)
    size = gate_ref.shape[0] // (2 * PARTS)
    total = len(weights) * PARTS

    def rows_of(part):
        return pl.ds(pl.multiple_of((parity * PARTS + part) * size, size), size)

    def push(src, array, slot, part, recv, device):
        pltpu.make_async_remote_copy(
            src_ref=src,
            dst_ref=w_ref.at[array * 3 + slot, rows_of(part)],
            send_sem=w_send,
            recv_sem=recv,
            device_id=device,
            device_id_type=MESH,
        ).start()

    def near(array, slot, part):
        return w_recv.at[(array * 3 + slot) * PARTS + part]

    def arrived(array, slot, part):
        block = w_ref.at[array * 3 + slot, rows_of(part)]
        pltpu.make_async_copy(block, block, near(array, slot, part)).wait()

    def first(k):
        part = lax.rem(k, PARTS)
        for array in range(len(weights)):

            @pl.when(lax.div(k, PARTS) == array)
            def _():
                for slot, step in ((1, 1), (0, -1)):
                    push(
                        weights[array].at[rows_of(part)], array, slot, part,
                        near(array, slot, part), relative(exp=step),
                    )

    def along(array, slot, part):
        push(
            w_ref.at[array * 3 + slot, rows_of(part)], array, slot, part, far_recv,
            relative(dp=1 - 2 * lax.rem(part, 2)),
        )

    def third(k):
        array, part = lax.div(k, PARTS), lax.rem(k, PARTS)
        arrived(array, 2, part)
        along(array, 2, part)

    def event(k, carried):
        array, part = lax.div(k, PARTS), lax.rem(k, PARTS)

        @pl.when(k + AHEAD < total)
        def _():
            first(k + AHEAD)

        odd = lax.rem(part, 2)
        arrived(array, 0, part)
        arrived(array, 1, part)
        slot = 1 - odd
        push(
            w_ref.at[array * 3 + slot, rows_of(part)], array, 2, part,
            near(array, 2, part), relative(exp=1 - 2 * odd),
        )
        along(array, 0, part)
        along(array, 1, part)

        @pl.when(k >= 2)
        def _():
            third(k - 2)

        return carried

    def begin(k, carried):
        first(k)
        return carried

    lax.fori_loop(0, AHEAD, begin, 0)
    lax.fori_loop(0, EARLY, event, 0)

    pltpu.make_async_copy(qkv, qkv, qkv_recv).wait()
    keys = qkv[1].reshape(length, width)
    kk[:, :width] = keys
    kk[:, width:] = keys
    vv[:, :width] = qkv[2].reshape(length, width)
    vv[:, width:] = jnp.ones((length, width), vv.dtype)

    per = bq // rows
    lam = lam_ref[me]

    blocks = length // bq
    start = lax.rem(lax.axis_index("ctx"), blocks)
    chunks = blocks * (blocks + 1) // 2

    def query_block(turn, carried):
        i = lax.rem(start + turn, blocks)
        done = EARLY + chunks * lax.div(start + turn, blocks)
        done = done + lax.div(i * (i + 1), 2) - lax.div(start * (start + 1), 2)

        def weight_step(j, phase):
            @pl.when(lax.rem(j, 2) == phase)
            def _():
                event(done + lax.div(j, 2) + phase * (lax.div(i, 2) + 1), 0)

        q = qkv[0, pl.ds(i * per, per)].reshape(bq, width)
        q = q.astype(jnp.float32) * (LOG2E / math.sqrt(half))
        hi = q.astype(jnp.bfloat16)
        lo = (q - hi.astype(jnp.float32)).astype(jnp.bfloat16)
        lower = lax.broadcasted_iota(jnp.int32, (bq, width), 1) < half
        zero = jnp.zeros((bq, width), jnp.bfloat16)
        qq[:bq, :width] = jnp.where(lower, hi, zero)
        qq[:bq, width:] = jnp.where(lower, lo, zero)
        qq[bq:, :width] = jnp.where(lower, zero, hi)
        qq[bq:, width:] = jnp.where(lower, zero, lo)
        acc[...] = jnp.zeros_like(acc)
        largest[...] = jnp.full_like(largest, LOW)

        def scores(j, masked):
            keys_here = pl.ds(pl.multiple_of(j * bk, bk), bk)
            s = lax.dot_general(
                qq[...], kk[keys_here, :], contract_last, preferred_element_type=jnp.float32
            )
            if masked:
                row = i * bq + lax.broadcasted_iota(jnp.int32, (bq, bk), 0)
                col = j * bk + lax.broadcasted_iota(jnp.int32, (bq, bk), 1)
                allowed = col <= row
                s = jnp.where(jnp.concatenate([allowed, allowed], axis=0), s, LOW)
            return s

        def look(j, masked):
            weight_step(j, 0)
            s = scores(j, masked)
            top = largest[...]
            for c in range(0, bk, width):
                top = jnp.maximum(top, s[:, c : c + width])
            largest[...] = top

        def add(j, masked):
            weight_step(j, 1)
            s = scores(j, masked)
            top = largest[...]
            raised = jnp.concatenate(
                [jnp.exp2(s[:, c : c + width] - top).astype(jnp.bfloat16) for c in range(0, bk, width)],
                axis=1,
            )
            keys_here = pl.ds(pl.multiple_of(j * bk, bk), bk)
            acc[...] += jnp.dot(raised, vv[keys_here, :], preferred_element_type=jnp.float32)

        full = lax.div(i * bq, bk)

        def look_body(j, inner):
            look(j, False)
            return inner

        def add_body(j, inner):
            add(j, False)
            return inner

        lax.fori_loop(0, full, look_body, 0)
        look(full, True)
        largest[...] = jnp.broadcast_to(
            jnp.max(largest[...], axis=1, keepdims=True), largest.shape
        )
        lax.fori_loop(0, full, add_body, 0)
        add(full, True)
        one = acc[:bq, :width] / acc[:bq, width:]
        two = acc[bq:, :width] / acc[bq:, width:]
        blend = one - lam * two
        mean = jnp.mean(blend * blend, axis=1, keepdims=True)
        out = (OUT_SCALE * blend * lax.rsqrt(mean + EPSILON)).astype(mixed.dtype)
        mixed[pl.ds(i * per, per)] = out.reshape(per, rows, width)

        def send_rows(r, inner):
            target = i * per + r

            @pl.when(target != me)
            def _():
                pltpu.make_async_remote_copy(
                    src_ref=mixed.at[target],
                    dst_ref=heads_ref.at[me],
                    send_sem=out_send,
                    recv_sem=out_recv,
                    device_id=member(target),
                    device_id_type=MESH,
                ).start()

            @pl.when(target == me)
            def _():
                pltpu.make_async_copy(mixed.at[target], heads_ref.at[me], out_recv).start()

            return inner

        lax.fori_loop(0, per, send_rows, 0)
        return carried

    lax.fori_loop(0, blocks, query_block, 0)
    lax.fori_loop(EARLY + chunks, EARLY + chunks + 2, event, 0)
    pltpu.make_async_copy(heads_ref, heads_ref, out_recv).wait()
    route(res_ref, heads_ref, router_ref, routes_ref, cap_ref, gates_ref, normed, buf)

    here = lax.axis_index("ctx")

    def send_expert(step, carried):
        target = lax.rem(here + step, experts)
        pltpu.make_async_remote_copy(
            src_ref=buf.at[target],
            dst_ref=x_ref.at[here],
            send_sem=x_send,
            recv_sem=x_recv,
            device_id=relative(ctx=step),
            device_id_type=MESH,
        ).start()
        return carried

    lax.fori_loop(1, experts, send_expert, 0)
    pltpu.make_async_copy(buf.at[here], x_ref.at[here], x_recv).start()

    lax.fori_loop(EARLY + chunks + 2, total, event, 0)
    third(total - 2)
    third(total - 1)
    others = pl.ds(0, sources - 1)
    for which in range(3):
        pltpu.make_async_copy(qkv.at[which, others], qkv.at[which, others], qkv_send).wait()
    pltpu.make_async_copy(mixed.at[others], mixed.at[others], out_send).wait()
    pltpu.make_async_copy(buf.at[pl.ds(1, experts - 1)], buf.at[pl.ds(1, experts - 1)], x_send).wait()
    pltpu.make_async_copy(x_ref, x_ref, x_recv).wait()
    halves = size * PARTS
    far = w_ref.at[:, pl.ds(pl.multiple_of((1 - parity) * halves, halves), halves)]
    pltpu.make_async_copy(far, far, far_recv).wait()
    pltpu.make_async_copy(w_ref, w_ref, w_send).wait()


def route(res_ref, heads_ref, router_ref, routes_ref, cap_ref, gates_ref, normed, buf):
    heads, tokens, width = heads_ref.shape
    experts, room, _ = buf.shape
    square = jnp.zeros((tokens, width), jnp.float32)
    for h in range(heads):
        block = attend_columns(res_ref, heads_ref, h)
        square = square + block * block
    mean = jnp.sum(square, axis=1, keepdims=True) / (heads * width)
    factor = lax.rsqrt(mean + EPSILON)
    for h in range(heads):
        block = attend_columns(res_ref, heads_ref, h)
        normed[:, h * width : (h + 1) * width] = (block * factor).astype(jnp.bfloat16)
    logits = lax.dot_general(
        router_ref[...], normed[...], contract_last, preferred_element_type=jnp.float32
    )
    sig = 1.0 / (1.0 + jnp.exp(-logits))
    expert_of = lax.broadcasted_iota(jnp.int32, (experts, tokens), 0)
    named = (routes_ref[0:1, :] == expert_of) | (routes_ref[1:2, :] == expert_of)
    picked = jnp.where(named, sig, 0.0)
    gates = picked / jnp.sum(picked, axis=0, keepdims=True)
    before = lax.broadcasted_iota(jnp.int32, (tokens, tokens), 0) < lax.broadcasted_iota(
        jnp.int32, (tokens, tokens), 1
    )
    position = jnp.dot(
        jnp.where(named, 1.0, 0.0).astype(jnp.bfloat16),
        jnp.where(before, 1.0, 0.0).astype(jnp.bfloat16),
        preferred_element_type=jnp.float32,
    )
    kept = named & (position < cap_ref[...].astype(jnp.float32))
    position = jnp.where(kept, position, -1.0).astype(jnp.int32)
    slot = lax.broadcasted_iota(jnp.int32, (room, tokens), 0)
    chosen = [slot == position[e : e + 1, :] for e in range(experts)]
    one_hot = jnp.concatenate([jnp.where(c, 1.0, 0.0) for c in chosen], axis=0).astype(jnp.bfloat16)
    gates_ref[...] = jnp.concatenate(
        [jnp.where(chosen[e][:SLOTS], gates[e : e + 1, :], 0.0) for e in range(experts)], axis=0
    )
    for column in range(0, heads * width, 512):
        columns = slice(column, column + 512)
        moved = jnp.dot(one_hot, normed[:, columns], preferred_element_type=jnp.float32)
        buf[:, :, columns] = moved.astype(jnp.bfloat16).reshape(experts, room, 512)


def front(lambdas, queries, key_rows, value_rows, own, residual, router, routes, capacity, bq=1024, bk=1024):
    rows, total = queries.shape
    experts = router.shape[0]
    width = LANES
    heads = total // width
    length = heads * rows
    anywhere = pl.BlockSpec(memory_space=pl.ANY)
    vmem = pl.BlockSpec(memory_space=pltpu.VMEM)
    slots = len(own) * (lax.axis_size("exp") - 1)
    dma = pltpu.SemaphoreType.DMA
    return pl.pallas_call(
        functools.partial(front_kernel, bq, bk),
        out_shape=(
            jax.ShapeDtypeStruct((heads, rows, width), jnp.bfloat16),
            jax.ShapeDtypeStruct((experts * SLOTS, rows), jnp.float32),
            jax.ShapeDtypeStruct((experts, ROOM, total), jnp.bfloat16),
            jax.ShapeDtypeStruct((slots, *own[0].shape), jnp.bfloat16),
        ),
        in_specs=[pl.BlockSpec(memory_space=pltpu.SMEM)] + [anywhere] * 6 + [vmem] * 4,
        out_specs=(vmem, vmem, anywhere, anywhere),
        scratch_shapes=[
            pltpu.VMEM((3, heads, rows, width), jnp.bfloat16),
            pltpu.VMEM((heads, rows, width), jnp.bfloat16),
            pltpu.VMEM((length, 2 * width), jnp.bfloat16),
            pltpu.VMEM((length, 2 * width), jnp.bfloat16),
            pltpu.VMEM((2 * bq, 2 * width), jnp.bfloat16),
            pltpu.VMEM((2 * bq, 2 * width), jnp.float32),
            pltpu.VMEM((2 * bq, width), jnp.float32),
            pltpu.VMEM((rows, total), jnp.bfloat16),
            pltpu.VMEM((experts, ROOM, total), jnp.bfloat16),
        ]
        + [dma] * 8
        + [dma((slots * PARTS,))],
        compiler_params=pltpu.CompilerParams(
            vmem_limit_bytes=58 * MIB, collective_id=0, has_side_effects=True
        ),
        name="front",
    )(lambdas, queries, key_rows, value_rows, *own, residual, router, routes, capacity)


def expert_kernel(x_ref, gate_own, up_own, down_own, gate_ref, up_ref, down_ref, o_ref, x_all, acc):
    group = pl.program_id(0)
    sources, _, width = x_ref.shape

    def contribute(gate_w, up_w, down_w, begin):
        x = x_all[...]
        gate_out = jnp.dot(x, gate_w[...], preferred_element_type=jnp.float32)
        up_out = jnp.dot(x, up_w[...], preferred_element_type=jnp.float32)
        hidden = (gate_out / (1.0 + jnp.exp(-gate_out)) * up_out).astype(jnp.bfloat16)
        for c in range(0, width, 512):
            part = lax.dot_general(
                hidden, down_w[c : c + 512, :], contract_last, preferred_element_type=jnp.float32
            ).astype(jnp.bfloat16).astype(jnp.float32)
            if begin:
                acc[:, c : c + 512] = part
            else:
                acc[:, c : c + 512] += part

    @pl.when(group == 0)
    def _():
        for c in range(0, width, 512):
            parts = [
                x_ref[s, :, c : c + 512].astype(jnp.float32)[:SLOTS] for s in range(sources)
            ]
            x_all[:, c : c + 512] = jnp.concatenate(parts, axis=0).astype(x_all.dtype)
        contribute(gate_own, up_own, down_own, True)

    @pl.when(group > 0)
    def _():
        contribute(gate_ref, up_ref, down_ref, False)

    @pl.when(group == pl.num_programs(0) - 1)
    def _():
        o_ref[...] = acc[...].astype(o_ref.dtype)


def expert(x, own, others):
    sources, room, width = x.shape
    rows = sources * SLOTS
    slots, _, hidden = others.shape
    arrays = len(own)
    each = slots // arrays
    whole = pl.BlockSpec((width, hidden), lambda g: (0, 0), pipeline_mode=pl.Buffered(1))

    def weight(array):
        return pl.BlockSpec(
            (None, width, hidden), lambda g: (array * each + jnp.maximum(g - 1, 0), 0, 0)
        )

    return pl.pallas_call(
        expert_kernel,
        grid=(each + 1,),
        out_shape=jax.ShapeDtypeStruct((rows, width), jnp.bfloat16),
        in_specs=[pl.BlockSpec((sources, room, width), lambda g: (0, 0, 0), pipeline_mode=pl.Buffered(1))]
        + [whole] * arrays
        + [weight(a) for a in range(arrays)],
        out_specs=pl.BlockSpec((rows, width), lambda g: (0, 0)),
        scratch_shapes=[pltpu.VMEM((rows, width), jnp.bfloat16), pltpu.VMEM((rows, width), jnp.float32)],
        compiler_params=pltpu.CompilerParams(vmem_limit_bytes=56 * MIB),
        name="experts",
    )(x, *own, others, others, others)


def combine_kernel(res_ref, heads_ref, back_ref, gate_ref, o_ref):
    heads = heads_ref.shape[0]
    gates = gate_ref[...]
    hi = gates.astype(jnp.bfloat16)
    lo = (gates - hi.astype(jnp.float32)).astype(jnp.bfloat16)
    for h in range(heads):
        columns = slice(h * LANES, (h + 1) * LANES)
        back = back_ref[:, columns]
        total = lax.dot_general(hi, back, contract_first, preferred_element_type=jnp.float32)
        total += lax.dot_general(lo, back, contract_first, preferred_element_type=jnp.float32)
        o_ref[:, columns] = (attend_columns(res_ref, heads_ref, h) + total).astype(o_ref.dtype)


def combine(residual, heads, back, gates):
    return pl.pallas_call(
        combine_kernel,
        out_shape=jax.ShapeDtypeStruct(residual.shape, jnp.bfloat16),
        compiler_params=pltpu.CompilerParams(vmem_limit_bytes=48 * MIB),
        name="combine",
    )(residual, heads, back, gates)


def shards(
    queries, key_rows, value_rows, residual, lambdas, router, gate_proj, up_proj, down_proj, routes, capacity
):
    tokens, width = queries.shape
    experts = router.shape[1]
    own = (gate_proj[0], up_proj[0], down_proj[0])
    mixed, gates, x, others = front(
        lambdas, queries, key_rows, value_rows, own, residual, router.T, routes.T, capacity.T
    )
    results = expert(x, own, others)
    back = lax.all_to_all(
        results.reshape(experts, SLOTS, width), "ctx", split_axis=0, concat_axis=0, tiled=True
    )
    return combine(residual, mixed, back.reshape(experts * SLOTS, width), gates)


def solution(mesh):
    rows = P(("dp", "ctx", "exp"), None)
    weights = P("ctx", None, "exp")
    placed = (rows, rows, rows, rows, P(), P(), weights, weights, weights, rows, rows)
    return jax.shard_map(shards, mesh=mesh, in_specs=placed, out_specs=rows, check_vma=False)
```
